32 devices in a mesh: rep: 4 (over y, x), mp: 8 (over z, core).
Axes of the slice: x: 2, y: 2, z: 4, core: 2. Of those that a mesh axis runs over, the one named last changes fastest.
Arguments:
- dense_feats: bfloat16 [4096, 13], P(('rep', 'mp')), may hold values from -6 to 6
- bag_counts: int32 [4096, 8, 64], P('rep', 'mp'), may hold values from 0 to 2
- emb_rows: bfloat16 [8, 64, 256], P('mp'), may hold values from -0.625 to 0.625
- v_emb: bfloat16 [2048, 256], P('mp'), may hold values from -0.125 to 0.125
- u_emb: bfloat16 [256, 2048], P(None, 'mp'), may hold values from -0.375 to 0.375
- b_emb: bfloat16 [2048], P('mp'), may hold values from -3 to 3
- v_bot: bfloat16 [256, 256], replicated, may hold values from -0.375 to 0.375
- u_bot: bfloat16 [256, 256], replicated, may hold values from -0.375 to 0.375
- b_bot: bfloat16 [256], replicated, may hold values from -3 to 3
- w_first: bfloat16 [13, 1024], replicated, may hold values from -1.75 to 1.75
- b_first: bfloat16 [1024], replicated, may hold values from -3 to 3
- w_second: bfloat16 [1024, 256], replicated, may hold values from -0.1875 to 0.1875
- b_second: bfloat16 [256], replicated, may hold values from -3 to 3
- cot_cross: bfloat16 [4096, 2048], P(('rep', 'mp')), may hold values from -12 to 12
- cot_bottom: bfloat16 [4096, 256], P(('rep', 'mp')), may hold values from -6 to 6
Outputs:
- cross_emb: bfloat16 [4096, 2048], P(('rep', 'mp'))
- cross_bot: bfloat16 [4096, 256], P(('rep', 'mp'))
- grad_table: bfloat16 [8, 64, 256], P('mp')
- grad_v_emb: bfloat16 [2048, 256], P('mp')
- grad_u_emb: bfloat16 [256, 2048], P(None, 'mp')
- grad_b_emb: bfloat16 [2048], P('mp')
- grad_v_bot: bfloat16 [256, 256], replicated
- grad_u_bot: bfloat16 [256, 256], replicated
- grad_b_bot: bfloat16 [256], replicated
- grad_w_first: bfloat16 [13, 1024], replicated
- grad_b_first: bfloat16 [1024], replicated
- grad_w_second: bfloat16 [1024, 256], replicated
- grad_b_second: bfloat16 [256], replicated
The draws below stay inside these ranges and needn't reach their ends.
Inputs may be any that keep to these rules, and one draw needn't show every extreme that they name: bag_counts[s, t, j] is how often row j of table t occurs in the bag of sample s.
All inputs are finite; a program needn't handle non-finite values.
Results may differ from the reference program's by a relative error of at most 0.029.
Values may be sent and summed in bfloat16 or wider, within the bound.
No kernel may reach another device: no remote copies, remote signals or barrier semaphores. Data moves between devices by JAX's collectives and lax.ppermute only.
A program may use at most 64 MiB of HBM per device.

```python
import math
import jax
import jax.numpy as jnp
from jax import lax

E = 256
R = 256
H = 1024
NUM_DENSE = 13
ROWS = 64
B_DEV = 128
TABLES = 8
F = 2048
SAMPLES = 4096
N_REP = 4
N_MP = 8


def touch_ends(values, own_key, least, high):
    extent = values.shape
    spot = [jax.random.randint(jax.random.fold_in(own_key, axis), (), 0, extent[axis]) for axis in range(len(extent))]
    values = values.at[tuple(spot)].set(least)
    longest = extent.index(max(extent))
    spot[longest] = (spot[longest] + 1) % extent[longest]
    return values.at[tuple(spot)].set(high)


def strengthened(drawn, own_key, source, target, shards_of, factor):
    owner, partner = [(jnp.arange(drawn.shape[axis_at]) // (drawn.shape[axis_at] // shards_of)).reshape([-1 if axis == axis_at else 1 for axis in range(drawn.ndim)]) for axis_at in (source, target)]
    chosen = jax.random.permutation(own_key, shards_of)[partner]
    strong = (owner == chosen) | (owner == (partner + shards_of // 2) % shards_of)
    return jnp.where(strong, factor * drawn, drawn)


def shard_levels(stream_key, dims, cuts, low, top_value):
    level, own = 1.0, jax.random.fold_in(stream_key, 6)
    for position, shards_of in cuts:
        draws = jnp.exp(jax.random.uniform(jax.random.fold_in(own, position), (shards_of,), jnp.float32, low / len(cuts), top_value / len(cuts)))
        level = level * jnp.repeat(draws, dims[position] // shards_of).reshape([-1 if axis == position else 1 for axis in range(len(dims))])
    return level


def scatter_about(stream_key, shape, deviation, reach, cuts=(), held_as=jnp.bfloat16):
    values = deviation * jax.random.normal(stream_key, shape, jnp.float32)
    if cuts:
        values = values * shard_levels(stream_key, shape, cuts, -0.22, 0.18)
    return jnp.clip(values, -reach, reach).astype(held_as)


def gaussian_with(rng, extent, scale, bound, cuts, heavy, held_as=jnp.bfloat16):
    entries = scale * jax.random.normal(rng, extent, jnp.float32)
    if cuts:
        entries = entries * shard_levels(rng, extent, cuts, -0.22, 0.18)
    return jnp.clip(strengthened(entries, jax.random.fold_in(rng, 3), *heavy), -bound, bound).astype(held_as)


def setup_inputs(seed: int = 0) -> dict:
    streams_of = jax.random.split(jax.random.key(seed), 16)
    return {
        "dense_feats": scatter_about(streams_of[0], (SAMPLES, NUM_DENSE), 1.0, 6.0, ((0, 32),)),
        "bag_counts": touch_ends(jax.random.randint(streams_of[1], (SAMPLES, TABLES, ROWS), 0, 3), jax.random.fold_in(streams_of[1], 1), 0, 2).astype(jnp.int32),
        "emb_rows": scatter_about(streams_of[2], (TABLES, ROWS, E), 0.1, 0.625, ((0, 8),)),
        "v_emb": scatter_about(streams_of[3], (F, R), F ** -0.5, 0.125, ((0, 8),)),
        "u_emb": scatter_about(streams_of[4], (R, F), R ** -0.5, 0.375, ((1, 8),)),
        "b_emb": scatter_about(streams_of[5], (F,), 0.5, 3.0, ((0, 8),)),
        "v_bot": scatter_about(streams_of[6], (E, R), E ** -0.5, 0.375),
        "u_bot": scatter_about(streams_of[7], (R, E), R ** -0.5, 0.375),
        "b_bot": scatter_about(streams_of[8], (E,), 0.5, 3.0),
        "w_first": scatter_about(streams_of[9], (NUM_DENSE, H), NUM_DENSE ** -0.5, 1.75),
        "b_first": scatter_about(streams_of[10], (H,), 0.5, 3.0),
        "w_second": scatter_about(streams_of[11], (H, E), H ** -0.5, 0.1875),
        "b_second": scatter_about(streams_of[12], (E,), 0.5, 3.0),
        "cot_cross": gaussian_with(streams_of[13], (SAMPLES, F), 1.0, 12.0, ((0, 32),), (0, 1, 32, 2.75)),
        "cot_bottom": scatter_about(streams_of[14], (SAMPLES, E), 1.0, 6.0, ((0, 32),)),
    }


def silu_slope(inputs):
    gate_value = jax.nn.sigmoid(inputs)
    return gate_value * (1.0 + inputs * (1.0 - gate_value))

def contract_rows(left_side, right_side):
    return lax.dot_general(left_side, right_side, (((0,), (0,)), ((), ())), preferred_element_type=jnp.float32)

def contract_cols(left_side, right_side):
    return lax.dot_general(left_side, right_side, (((1,), (1,)), ((), ())), preferred_element_type=jnp.float32)

def rounded(values):
    return lax.optimization_barrier(values.astype(jnp.bfloat16)).astype(jnp.float32)

def reference(dense_feats, bag_counts, emb_rows, v_emb, u_emb, b_emb, v_bot, u_bot, b_bot, w_first, b_first, w_second, b_second, cot_cross, cot_bottom):
    group_rows = B_DEV * N_MP
    grad_scale = 1.0 / math.sqrt(SAMPLES)
    first_pre = jnp.dot(dense_feats, w_first, preferred_element_type=jnp.float32) + b_first.astype(jnp.float32)
    first_act = jax.nn.silu(first_pre).astype(jnp.bfloat16)
    second_pre = jnp.dot(first_act, w_second, preferred_element_type=jnp.float32) + b_second.astype(jnp.float32)
    bottom = jax.nn.silu(second_pre).astype(jnp.bfloat16)
    emb_full = emb_rows.astype(jnp.float32)
    v_blocks = v_emb.astype(jnp.float32).reshape(TABLES, E, R)
    u_blocks = u_emb.astype(jnp.float32).reshape(R, TABLES, E)
    b_blocks = b_emb.astype(jnp.float32).reshape(TABLES, E)
    owner_mask = (jnp.arange(TABLES)[:, None] == jnp.arange(group_rows)[None, :] // B_DEV).astype(jnp.float32)
    grad_table = jnp.zeros((TABLES, ROWS, E), jnp.float32)
    grad_v = jnp.zeros((TABLES, E, R), jnp.float32)
    grad_u = jnp.zeros((R, TABLES, E), jnp.float32)
    grad_b = jnp.zeros((TABLES, E), jnp.float32)
    grad_vb = jnp.zeros((E, R), jnp.float32)
    grad_ub = jnp.zeros((R, E), jnp.float32)
    grad_bb = jnp.zeros((E,), jnp.float32)
    grad_ws = jnp.zeros((H, E), jnp.float32)
    grad_bs = jnp.zeros((E,), jnp.float32)
    grad_wf = jnp.zeros((NUM_DENSE, H), jnp.float32)
    grad_bf = jnp.zeros((H,), jnp.float32)
    cross_parts = []
    bottom_parts = []
    for replica in range(N_REP):
        lower = replica * group_rows
        upper = lower + group_rows
        counts = bag_counts[lower:upper].astype(jnp.float32)
        pooled = rounded(jnp.einsum('stj,tje->tse', counts, emb_full))
        bottom_rows = bottom[lower:upper]
        bottom_full = bottom_rows.astype(jnp.float32)
        bottom_term = jnp.dot(bottom_rows, v_bot, preferred_element_type=jnp.float32)
        low_terms = jnp.einsum('tse,ter->tsr', pooled, v_blocks) + owner_mask[:, :, None] * bottom_term[None]
        low_rank = lax.optimization_barrier(jnp.sum(rounded(low_terms), axis=0)).astype(jnp.bfloat16)
        low_full = low_rank.astype(jnp.float32)
        lift_emb = jnp.einsum('sr,rte->tse', low_full, u_blocks) + b_blocks[:, None, :]
        cross_rows = (pooled * (lift_emb + 1.0)).astype(jnp.bfloat16)
        cross_parts.append(jnp.transpose(cross_rows, (1, 0, 2)).reshape(group_rows, TABLES * E))
        lift_bottom = jnp.dot(low_rank, u_bot, preferred_element_type=jnp.float32) + b_bot.astype(jnp.float32)
        bottom_parts.append((bottom_full * (lift_bottom + 1.0)).astype(jnp.bfloat16))
        cot_rows = jnp.transpose(cot_cross[lower:upper].astype(jnp.float32).reshape(group_rows, TABLES, E), (1, 0, 2))
        d_lift = cot_rows * pooled
        d_lift_round = rounded(d_lift)
        cot_low = cot_bottom[lower:upper].astype(jnp.float32)
        d_bottom_lift = cot_low * bottom_full
        d_bottom_round = d_bottom_lift.astype(jnp.bfloat16)
        back_terms = jnp.einsum('tse,rte->tsr', d_lift_round, u_blocks)
        d_low = (lax.optimization_barrier(jnp.sum(rounded(back_terms), axis=0)) + contract_cols(d_bottom_round, u_bot)).astype(jnp.bfloat16)
        d_low_full = d_low.astype(jnp.float32)
        d_pooled = rounded(cot_rows * (lift_emb + 1.0) + jnp.einsum('sr,ter->tse', d_low_full, v_blocks))
        grad_table = grad_table + grad_scale * jnp.einsum('stj,tse->tje', counts, d_pooled)
        grad_v = grad_v + grad_scale * jnp.einsum('tse,sr->ter', pooled, d_low_full)
        grad_u = grad_u + grad_scale * jnp.einsum('sr,tse->rte', low_full, d_lift_round)
        grad_b = grad_b + grad_scale * lax.optimization_barrier(jnp.sum(d_lift, axis=1))
        d_bottom = cot_low * (lift_bottom + 1.0) + contract_cols(d_low, v_bot)
        grad_vb = grad_vb + grad_scale * contract_rows(bottom_rows, d_low)
        grad_ub = grad_ub + grad_scale * contract_rows(low_rank, d_bottom_round)
        grad_bb = grad_bb + grad_scale * lax.optimization_barrier(jnp.sum(d_bottom_lift, axis=0))
        d_second = d_bottom * silu_slope(second_pre[lower:upper])
        d_second_round = d_second.astype(jnp.bfloat16)
        grad_ws = grad_ws + grad_scale * contract_rows(first_act[lower:upper], d_second_round)
        grad_bs = grad_bs + grad_scale * lax.optimization_barrier(jnp.sum(d_second, axis=0))
        d_first = contract_cols(d_second_round, w_second) * silu_slope(first_pre[lower:upper])
        d_first_round = d_first.astype(jnp.bfloat16)
        grad_wf = grad_wf + grad_scale * contract_rows(dense_feats[lower:upper], d_first_round)
        grad_bf = grad_bf + grad_scale * lax.optimization_barrier(jnp.sum(d_first, axis=0))
    cross_emb = jnp.concatenate(cross_parts, axis=0)
    cross_bot = jnp.concatenate(bottom_parts, axis=0)
    return (cross_emb, cross_bot, grad_table.astype(jnp.bfloat16), grad_v.reshape(TABLES * E, R).astype(jnp.bfloat16), grad_u.reshape(R, TABLES * E).astype(jnp.bfloat16), grad_b.reshape(TABLES * E).astype(jnp.bfloat16), grad_vb.astype(jnp.bfloat16), grad_ub.astype(jnp.bfloat16), grad_bb.astype(jnp.bfloat16), grad_wf.astype(jnp.bfloat16), grad_bf.astype(jnp.bfloat16), grad_ws.astype(jnp.bfloat16), grad_bs.astype(jnp.bfloat16))
```

```python
import math

import jax
import jax.numpy as jnp
from jax import lax
from jax.experimental import pallas as pl
from jax.experimental.pallas import tpu as pltpu
from jax.sharding import Mesh
from jax.sharding import PartitionSpec as P

BF = jnp.bfloat16
F32 = jnp.float32
TILE = 16


def round_up(value, unit):
    return -(-value // unit) * unit


def silu_parts(inputs):
    gate_value = jax.nn.sigmoid(inputs)
    return inputs * gate_value, gate_value * (1.0 + inputs * (1.0 - gate_value))


def mul_nn(left, right):
    return lax.dot_general(left, right, (((1,), (0,)), ((), ())), preferred_element_type=F32)


def mul_tn(left, right):
    return lax.dot_general(left, right, (((0,), (0,)), ((), ())), preferred_element_type=F32)


def mul_nt(left, right):
    return lax.dot_general(left, right, (((1,), (1,)), ((), ())), preferred_element_type=F32)


def tree_sum(values):
    while len(values) > 1:
        values = [a + b for a, b in zip(values[::2], values[1::2])]
    return values[0]


def rows_of(index, count):
    return pl.ds(pl.multiple_of(index * count, TILE), count)


def cols_of(index, count):
    return pl.ds(pl.multiple_of(index * count, 128), count)


def run(body, out_shapes, args, name, scratch=(), flops=10**8, limit=6):
    in_vmem = pl.BlockSpec(memory_space=pltpu.VMEM)
    moved = sum(math.prod(a.shape) * a.dtype.itemsize for a in (*args, *out_shapes))

    def placed(spot_ref, *refs):
        body((spot_ref[0], spot_ref[1], spot_ref[2]), *refs)

    return pl.pallas_call(
        placed,
        out_shape=out_shapes,
        in_specs=[pl.BlockSpec(memory_space=pltpu.SMEM)] + [in_vmem] * (len(args) - 1),
        out_specs=[in_vmem] * len(out_shapes),
        scratch_shapes=list(scratch),
        compiler_params=pltpu.CompilerParams(vmem_limit_bytes=limit * 2**20),
        cost_estimate=pl.CostEstimate(flops=flops, bytes_accessed=moved, transcendentals=0),
        name=name,
    )(*args)


def shape(rows, cols, dtype=BF):
    return jax.ShapeDtypeStruct((rows, cols), dtype)


def local(
    dense_feats,
    bag_counts,
    emb_rows,
    v_emb,
    u_emb,
    b_emb,
    v_bot,
    u_bot,
    b_bot,
    w_first,
    b_first,
    w_second,
    b_second,
    cot_cross,
    cot_bottom,
):
    n_rep, n_z = lax.axis_size("rep"), lax.axis_size("z")
    own_rows, n_feat = dense_feats.shape
    hidden = w_first.shape[1]
    width = v_bot.shape[0]
    n_bag = bag_counts.shape[2]
    pair = 2 * own_rows
    grad_scale = 1.0 / math.sqrt(own_rows * 2 * n_z * n_rep)
    u_part = width // n_rep
    bag_part = round_up(-(-2 * n_bag // n_rep), TILE)
    bag_full = bag_part * n_rep
    dense_rows = hidden + 2 * width
    dense_part = round_up(-(-dense_rows // (2 * n_rep)), TILE)
    feat_rows = round_up(n_feat + 1, TILE)
    n_wide = hidden // width
    slots = [(q * feat_rows + i) for i in range(n_feat + 1, feat_rows) for q in range(n_wide)]
    small_rows = n_wide * feat_rows
    while len(slots) < 2 + n_z:
        slots += list(range(small_rows, small_rows + TILE))
        small_rows += TILE
    small_rows = round_up(small_rows, TILE * n_rep)
    small_part = small_rows // n_rep
    rep_part = dense_part + small_part
    half = rep_part * n_rep
    z_rows = rep_part + u_part + bag_part
    msg_rows = 3 * n_bag + TILE
    gb_rows = round_up(n_z, 8)

    def swap(value):
        return lax.ppermute(value, "core", [(0, 1), (1, 0)])

    def to_z(value, k):
        return lax.ppermute(value, "z", [(i, i ^ k) for i in range(n_z)])

    def to_rep(value, k):
        return lax.ppermute(value, "rep", [(i, i ^ k) for i in range(n_rep)])

    def call(body, out_shapes, args, name, scratch=()):
        return run(body, out_shapes, (spots, *args), name, scratch)

    spots = jnp.stack([lax.axis_index(name) for name in ("rep", "z", "core")]).astype(jnp.int32)

    bias_rows = jnp.concatenate(
        [b[None].astype(F32) for b in (b_emb, b_second, b_bot)] + [jnp.zeros((5, width), F32)]
    )

    def bags_body(spot, ct_ref, emb_ref, v_ref, b_ref, *outs):
        _, z, c = spot
        emb = emb_ref[...]
        emb_v = mul_nn(emb, v_ref[...]).astype(BF)
        bias = jnp.broadcast_to(b_ref[0:1, :], (TILE, width)).astype(BF)
        for k, out in enumerate(outs):
            first = (z ^ k) * 2
            out[:n_bag, :own_rows] = ct_ref[:, cols_of(first + c, own_rows)].astype(F32).astype(BF)
            out[:n_bag, own_rows:] = (
                ct_ref[:, cols_of(first + 1 - c, own_rows)].astype(F32).astype(BF)
            )
            out[n_bag : 2 * n_bag, :] = emb
            out[2 * n_bag : 3 * n_bag, :] = emb_v
            out[3 * n_bag :, :] = bias

    counts_t = jnp.transpose(bag_counts, (1, 2, 0))[0]
    bags = call(
        bags_body,
        [shape(msg_rows, pair)] * n_z,
        (counts_t, emb_rows[0], v_emb, bias_rows),
        "bags",
    )
    bags = [bags[0]] + [to_z(bags[k], k) for k in range(1, n_z)]
    u_z = [u_emb] + [to_z(u_emb, k) for k in range(1, n_z)]

    def cot_body(spot, cot_ref, out):
        _, _, c = spot
        for t in range(n_z):
            out[:, t * width : (t + 1) * width] = cot_ref[:, cols_of(2 * t + 1 - c, width)]

    (cot_out,) = call(cot_body, [shape(own_rows, n_z * width)], (cot_cross,), "cot_send")
    cot_in = swap(cot_out)

    feats_t = jnp.concatenate(
        [
            dense_feats.T,
            jnp.ones((1, own_rows), BF),
            jnp.zeros((feat_rows - n_feat - 1, own_rows), BF),
        ]
    )
    first_rows = jnp.concatenate(
        [w_first, b_first[None], jnp.zeros((feat_rows - n_feat - 1, hidden), BF)]
    )

    def mlp_body(
        spot, x_ref, w1_ref, w2_ref, b_ref, vb_ref, ub_ref, cot_ref,
        act_ref, slope1_ref, bottom_ref, slope2_ref, term_ref, back_ref,
    ):
        act, slope1_ref[...] = silu_parts(mul_tn(x_ref[...], w1_ref[...]))
        act = act.astype(BF)
        act_ref[...] = act
        bottom, slope2_ref[...] = silu_parts(mul_nn(act, w2_ref[...]) + b_ref[1:2, :])
        bottom = bottom.astype(BF)
        bottom_ref[...] = bottom
        term_ref[...] = mul_nn(bottom, vb_ref[...])
        d_lift = (cot_ref[...].astype(F32) * bottom.astype(F32)).astype(BF)
        back_ref[...] = mul_nt(d_lift, ub_ref[...])

    act, slope1, bottom, slope2, bot_term, bot_back = call(
        mlp_body,
        [
            shape(own_rows, hidden),
            shape(own_rows, hidden, F32),
            shape(own_rows, width),
            shape(own_rows, width, F32),
            shape(own_rows, width, F32),
            shape(own_rows, width, F32),
        ],
        (feats_t, first_rows, w_second, bias_rows, v_bot, u_bot, cot_bottom),
        "mlp_forward",
    )

    def cot_of(cot_ref, cot_in_ref, zk, c):
        return jnp.concatenate(
            [cot_ref[:, cols_of(2 * zk + c, width)], cot_in_ref[:, cols_of(zk, width)]], axis=0
        ).astype(F32)

    def low_body(spot, *refs):
        bag = refs[:n_z]
        term_ref, part_ref, pooled_ref = refs[n_z:]
        low = jnp.zeros((pair, width), F32)
        for k in range(n_z):
            base = k * width
            counts = bag[k][:n_bag, :]
            pooled = mul_tn(counts, bag[k][n_bag : 2 * n_bag, :]).astype(BF)
            low += mul_tn(counts, bag[k][2 * n_bag : 3 * n_bag, :])
            pooled_ref[base : base + width, :] = pooled
        part_ref[:own_rows, :] = (low[:own_rows] + term_ref[...]).astype(BF)
        part_ref[own_rows:pair, :] = low[own_rows:].astype(BF)

    low_part, pooled = call(
        low_body, [shape(pair, width), shape(n_z * pair, width)], (*bags, bot_term), "low_terms"
    )
    low_in = swap(low_part)

    def summed(part_ref, in_ref):
        own = part_ref[:own_rows, :].astype(F32) + in_ref[own_rows:, :].astype(F32)
        other = part_ref[own_rows:, :].astype(F32) + in_ref[:own_rows, :].astype(F32)
        return own.astype(BF), other.astype(BF)

    def u_grad_body(spot, part_ref, in_ref, pooled_ref, cot_ref, cot_in_ref, low_ref, lift_ref, gb_ref, *outs):
        r, z, c = spot
        *outs, stack = outs
        low_ref[:own_rows, :], low_ref[own_rows:, :] = summed(part_ref, in_ref)
        low = low_ref[...]
        gb_ref[...] = jnp.zeros_like(gb_ref)
        for k in range(n_z):
            base = k * width
            pooled_full = pooled_ref[base : base + width, :].astype(F32)
            d_lift = cot_of(cot_ref, cot_in_ref, z ^ k, c) * pooled_full
            gb_ref[k : k + 1, :] = jnp.sum(d_lift, axis=0, keepdims=True) * grad_scale
            d_lift = d_lift.astype(BF)
            lift_ref[base : base + width, :] = d_lift
            stack[...] = (mul_tn(low, d_lift) * grad_scale).astype(BF)
            for j, out in enumerate(outs):
                out[k * u_part : (k + 1) * u_part, :] = stack[rows_of(r ^ j, u_part), :]

    low, d_lift, grad_b, *u_outs = call(
        u_grad_body,
        [shape(pair, width), shape(n_z * pair, width), shape(gb_rows, width, F32)]
        + [shape(n_z * u_part, width)] * n_rep,
        (low_part, low_in, pooled, cot_cross, cot_in),
        "u_grads",
        [pltpu.VMEM((width, width), BF)],
    )
    u_ins = [u_outs[0]] + [to_rep(u_outs[j], j) for j in range(1, n_rep)]

    def back_body(spot, *refs):
        u_refs = refs[:n_z]
        lift_ref, back_ref, part_ref = refs[n_z:]
        back = jnp.zeros((pair, width), F32)
        for k in range(n_z):
            back += mul_nt(lift_ref[k * width : (k + 1) * width, :], u_refs[k][...])
        part_ref[:own_rows, :] = (back[:own_rows] + back_ref[...]).astype(BF)
        part_ref[own_rows:pair, :] = back[own_rows:].astype(BF)

    (back_part,) = call(back_body, [shape(pair, width)], (*u_z, d_lift, bot_back), "back_terms")
    back_in = swap(back_part)

    def dense_body(
        spot, low_ref, part_ref, in_ref, act_ref, slope1_ref, bottom_ref, slope2_ref, cot_ref, x_ref,
        w2_ref, vb_ref, ub_ref, b_ref, gb_ref,
        cross_ref, send_ref, keep_ref, pack, small,
    ):
        _, z, c = spot
        low = low_ref[:own_rows, :]
        d_low, _ = summed(part_ref, in_ref)
        bottom = bottom_ref[...]
        bottom_full = bottom.astype(F32)
        cot = cot_ref[...].astype(F32)
        lift = mul_nn(low, ub_ref[...]) + b_ref[2:3, :] + 1.0
        cross_ref[...] = (bottom_full * lift).astype(BF)
        d_second = (cot * lift + mul_nt(d_low, vb_ref[...])) * slope2_ref[...]
        d_second_round = d_second.astype(BF)
        d_first = mul_nt(d_second_round, w2_ref[...]) * slope1_ref[...]
        d_bias = cot * bottom_full
        pack[...] = jnp.zeros_like(pack)

        def put(first, value):
            value = (value * grad_scale).astype(BF)
            at, last = first, first + value.shape[0]
            while at < last:
                block = at // dense_part
                end = min(last, (block + 1) * dense_part)
                start = block * rep_part + at - block * dense_part
                pack[start : start + end - at, :] = value[at - first : end - first]
                at = end

        put(0, mul_tn(act_ref[...], d_second_round))
        put(hidden, mul_tn(bottom, d_low))
        put(hidden + width, mul_tn(low, d_bias.astype(BF)))
        small[...] = jnp.zeros_like(small)
        g_first = mul_nn(x_ref[...], d_first.astype(BF)) * grad_scale
        for q in range(n_wide):
            small[q * feat_rows : (q + 1) * feat_rows, :] = g_first[
                :, q * width : (q + 1) * width
            ]
        small[slots[0] : slots[0] + 1, :] = jnp.sum(d_second, axis=0, keepdims=True) * grad_scale
        small[slots[1] : slots[1] + 1, :] = jnp.sum(d_bias, axis=0, keepdims=True) * grad_scale
        for slot in slots[2:]:
            small[slot : slot + 1, :] = jnp.zeros((1, width), F32)

        def put_small(which):
            for j in range(n_rep):
                start = pl.multiple_of((which * n_rep + j) * rep_part + dense_part, TILE)
                pack[pl.ds(start, small_part), :] = small[
                    j * small_part : (j + 1) * small_part, :
                ].astype(BF)

        put_small(1 - c)
        send_ref[...] = pack[rows_of(1 - c, half), :]
        for k in range(n_z):
            for t in range(n_z):

                @pl.when((z ^ k) == t)
                def _():
                    small[slots[2 + t] : slots[2 + t] + 1, :] = gb_ref[k : k + 1, :]

        put_small(c)
        keep_ref[...] = pack[rows_of(c, half), :]

    cross_bot, dense_out, dense_keep = call(
        dense_body,
        [shape(own_rows, width), shape(half, width), shape(half, width)],
        (
            low, back_part, back_in, act, slope1, bottom, slope2, cot_bottom, feats_t,
            w_second, v_bot, u_bot, bias_rows, grad_b,
        ),
        "dense_grads",
        [pltpu.VMEM((2 * half, width), BF), pltpu.VMEM((small_rows, width), F32)],
    )
    dense_in = swap(dense_out)

    def table_body(spot, *refs):
        bag = refs[:n_z]
        u_refs = refs[n_z : 2 * n_z]
        low_ref, part_ref, in_ref, pooled_ref, cot_ref, cot_in_ref = refs[2 * n_z : 2 * n_z + 6]
        own_ref, send_ref, out = refs[2 * n_z + 6 :]
        _, z, c = spot
        low = low_ref[...]
        d_low = jnp.concatenate(summed(part_ref, in_ref), axis=0)
        if bag_full > 2 * n_bag:
            out[...] = jnp.zeros_like(out)
        for k in range(n_z):
            base = k * width
            counts = bag[k][:n_bag, :]
            bias = bag[k][3 * n_bag :, :].astype(F32)[0:1]
            lift = mul_nn(low, u_refs[k][...]) + bias + 1.0
            cross = (pooled_ref[base : base + width, :].astype(F32) * lift).astype(BF)
            own_ref[:, cols_of(z ^ k, width)] = cross[:own_rows]
            send_ref[:, cols_of(z ^ k, width)] = cross[own_rows:]
            direct = (cot_of(cot_ref, cot_in_ref, z ^ k, c) * lift).astype(BF)
            start = k * bag_full
            out[start : start + n_bag, :] = (mul_nn(counts, d_low) * grad_scale).astype(BF)
            out[start + n_bag : start + 2 * n_bag, :] = (
                mul_nn(counts, direct) * grad_scale
            ).astype(BF)

    cross_own, cross_out, bag_keep = call(
        table_body,
        [shape(own_rows, n_z * width)] * 2 + [shape(n_z * bag_full, width)],
        (*bags, *u_z, low, back_part, back_in, pooled, cot_cross, cot_in),
        "table_grads",
    )

    def pair_body(spot, keep_ref, in_ref, bag_ref, *outs):
        r, _, _ = spot
        for j, out in enumerate(outs):
            rows = rows_of(r ^ j, rep_part)
            out[:rep_part, :] = (
                keep_ref[rows, :].astype(F32) + in_ref[rows, :].astype(F32)
            ).astype(BF)
            for k in range(n_z):
                rows = pl.ds(pl.multiple_of(k * bag_full + (r ^ j) * bag_part, TILE), bag_part)
                start = rep_part + k * bag_part
                out[start : start + bag_part, :] = bag_ref[rows, :]

    rep_outs = call(
        pair_body,
        [shape(rep_part + n_z * bag_part, width)] * n_rep,
        (dense_keep, dense_in, bag_keep),
        "pair_sum",
    )
    rep_ins = [rep_outs[0]] + [to_rep(rep_outs[j], j) for j in range(1, n_rep)]
    cross_in = swap(cross_out)

    def total(refs, first, count):
        return tree_sum([ref[first : first + count, :].astype(F32) for ref in refs]).astype(BF)

    def rep_body(spot, *refs):
        ins, u_refs, outs = refs[:n_rep], refs[n_rep : 2 * n_rep], refs[2 * n_rep :]
        dense = total(ins, 0, rep_part)
        for k, out in enumerate(outs):
            out[:rep_part, :] = dense
            out[rep_part : rep_part + u_part, :] = total(u_refs, k * u_part, u_part)
            out[rep_part + u_part :, :] = total(ins, rep_part + k * bag_part, bag_part)

    z_outs = call(rep_body, [shape(z_rows, width)] * n_z, (*rep_ins, *u_ins), "rep_sum")
    z_ins = [z_outs[0]] + [to_z(z_outs[k], k) for k in range(1, n_z)]

    def z_body(spot, *refs):
        refs[n_z][...] = total(refs[:n_z], 0, z_rows)

    (mine,) = call(z_body, [shape(z_rows, width)], z_ins, "z_sum")

    pieces = [mine] + [to_rep(mine, j) for j in range(1, n_rep)]

    def gather_body(spot, *refs):
        r, _, _ = spot
        for j in range(n_rep):
            refs[n_rep][rows_of(r ^ j, dense_part), :] = refs[j][:dense_part, :]

    (dense_own,) = call(gather_body, [shape(n_rep * dense_part, width)], pieces, "dense_gather")
    dense_other = swap(dense_own)

    def cross_body(spot, own_ref, in_ref, out):
        _, _, c = spot
        for t in range(n_z):
            cols = slice(t * width, (t + 1) * width)
            out[:, cols_of(2 * t + c, width)] = own_ref[:, cols]
            out[:, cols_of(2 * t + 1 - c, width)] = in_ref[:, cols]

    (cross_emb,) = call(
        cross_body, [shape(own_rows, 2 * n_z * width)], (cross_own, cross_in), "cross_rows"
    )

    def table_last_body(spot, *refs):
        ins = refs[:n_rep]
        emb_ref, v_ref, g_table, g_v, g_u, g_wide, g_rows, stack, small = refs[n_rep:]
        r, z, _ = spot
        for j in range(n_rep):
            rows = slice(rep_part, rep_part + u_part)
            g_u[rows_of(r ^ j, u_part), :] = ins[j][rows, :]
            stack[rows_of(r ^ j, bag_part), :] = ins[j][rep_part + u_part :, :]
            small[rows_of(r ^ j, small_part), :] = ins[j][dense_part:rep_part, :].astype(F32)
        bag_low = stack[:n_bag, :]
        g_v[...] = mul_tn(emb_ref[...], bag_low).astype(BF)
        direct = stack[n_bag : 2 * n_bag, :].astype(F32)
        g_table[...] = (direct + mul_nt(bag_low, v_ref[...])).astype(BF)
        for q in range(n_wide):
            g_wide[:, q * width : (q + 1) * width] = small[q * feat_rows : (q + 1) * feat_rows, :]
        g_rows[...] = jnp.zeros_like(g_rows)
        for i in range(2):
            g_rows[i : i + 1, :] = small[slots[i] : slots[i] + 1, :]
        for t in range(n_z):

            @pl.when(z == t)
            def _():
                g_rows[2:3, :] = small[slots[2 + t] : slots[2 + t] + 1, :]

    grad_table, grad_v, grad_u, g_wide, g_rows = call(
        table_last_body,
        [
            shape(n_bag, width),
            shape(width, width),
            shape(width, width),
            shape(feat_rows, hidden, F32),
            shape(8, width, F32),
        ],
        (*pieces, emb_rows[0], v_emb),
        "table_last",
        [pltpu.VMEM((bag_full, width), BF), pltpu.VMEM((small_rows, width), F32)],
    )
    g_wide, g_rows = g_wide.astype(BF), g_rows.astype(BF)

    def dense_last_body(spot, own_ref, other_ref, g_second, g_vb, g_ub, stack):
        _, _, c = spot
        stack[rows_of(c, n_rep * dense_part), :] = own_ref[...]
        stack[rows_of(1 - c, n_rep * dense_part), :] = other_ref[...]
        g_second[...] = stack[:hidden, :]
        g_vb[...] = stack[hidden : hidden + width, :]
        g_ub[...] = stack[hidden + width : dense_rows, :]

    grad_ws, grad_vb, grad_ub = call(
        dense_last_body,
        [shape(hidden, width), shape(width, width), shape(width, width)],
        (dense_own, dense_other),
        "dense_last",
        [pltpu.VMEM((2 * n_rep * dense_part, width), BF)],
    )
    return (
        cross_emb,
        cross_bot,
        grad_table[None],
        grad_v,
        grad_u,
        g_rows[2],
        grad_vb,
        grad_ub,
        g_rows[1],
        g_wide[:n_feat],
        g_wide[n_feat],
        grad_ws,
        g_rows[0],
    )


def solution(mesh):
    n_rep, n_mp = mesh.devices.shape
    mesh = Mesh(mesh.devices.reshape(n_rep, n_mp // 2, 2), ("rep", "z", "core"))
    return jax.shard_map(
        local,
        mesh=mesh,
        in_specs=(
            P(("rep", "z", "core"), None),
            P("rep", ("z", "core"), None),
            P(("z", "core"), None, None),
            P(("z", "core"), None),
            P(None, ("z", "core")),
            P(("z", "core")),
            P(),
            P(),
            P(),
            P(),
            P(),
            P(),
            P(),
            P(("rep", "z", "core"), None),
            P(("rep", "z", "core"), None),
        ),
        out_specs=(
            P(("rep", "z", "core"), None),
            P(("rep", "z", "core"), None),
            P(("z", "core"), None, None),
            P(("z", "core"), None),
            P(None, ("z", "core")),
            P(("z", "core")),
            P(),
            P(),
            P(),
            P(),
            P(),
            P(),
            P(),
        ),
        check_vma=False,
    )
```

```python
import math

import jax
import jax.numpy as jnp
from jax import lax
from jax.experimental import pallas as pl
from jax.experimental.pallas import tpu as pltpu
from jax.sharding import Mesh
from jax.sharding import PartitionSpec as P

BF = jnp.bfloat16
F32 = jnp.float32
TILE = 16


def round_up(value, unit):
    return -(-value // unit) * unit


def silu_parts(inputs):
    gate_value = jax.nn.sigmoid(inputs)
    return inputs * gate_value, gate_value * (1.0 + inputs * (1.0 - gate_value))


def mul_nn(left, right):
    return lax.dot_general(left, right, (((1,), (0,)), ((), ())), preferred_element_type=F32)


def mul_tn(left, right):
    return lax.dot_general(left, right, (((0,), (0,)), ((), ())), preferred_element_type=F32)


def mul_nt(left, right):
    return lax.dot_general(left, right, (((1,), (1,)), ((), ())), preferred_element_type=F32)


def tree_sum(values):
    while len(values) > 1:
        values = [a + b for a, b in zip(values[::2], values[1::2])]
    return values[0]


def rows_of(index, count):
    return pl.ds(pl.multiple_of(index * count, TILE), count)


def cols_of(index, count):
    return pl.ds(pl.multiple_of(index * count, 128), count)


def run(body, out_shapes, args, name, scratch=(), flops=10**8, limit=6):
    in_vmem = pl.BlockSpec(memory_space=pltpu.VMEM)
    moved = sum(math.prod(a.shape) * a.dtype.itemsize for a in (*args, *out_shapes))

    def placed(spot_ref, *refs):
        body((spot_ref[0, 0], spot_ref[1, 0], spot_ref[2, 0]), *refs)

    return pl.pallas_call(
        placed,
        out_shape=out_shapes,
        in_specs=[in_vmem] * len(args),
        out_specs=[in_vmem] * len(out_shapes),
        scratch_shapes=list(scratch),
        compiler_params=pltpu.CompilerParams(vmem_limit_bytes=limit * 2**20),
        cost_estimate=pl.CostEstimate(flops=flops, bytes_accessed=moved, transcendentals=0),
        name=name,
    )(*args)


def shape(rows, cols, dtype=BF):
    return jax.ShapeDtypeStruct((rows, cols), dtype)


def local(
    dense_feats,
    bag_counts,
    emb_rows,
    v_emb,
    u_emb,
    b_emb,
    v_bot,
    u_bot,
    b_bot,
    w_first,
    b_first,
    w_second,
    b_second,
    cot_cross,
    cot_bottom,
):
    n_rep, n_z = lax.axis_size("rep"), lax.axis_size("z")
    own_rows, n_feat = dense_feats.shape
    hidden = w_first.shape[1]
    width = v_bot.shape[0]
    n_bag = bag_counts.shape[2]
    pair = 2 * own_rows
    grad_scale = 1.0 / math.sqrt(own_rows * 2 * n_z * n_rep)
    u_part = width // n_rep
    bag_part = round_up(-(-2 * n_bag // n_rep), TILE)
    bag_full = bag_part * n_rep
    dense_rows = hidden + 2 * width
    dense_part = round_up(-(-dense_rows // (2 * n_rep)), TILE)
    feat_rows = round_up(n_feat + 1, TILE)
    n_wide = hidden // width
    slots = [(q * feat_rows + i) for i in range(n_feat + 1, feat_rows) for q in range(n_wide)]
    small_rows = n_wide * feat_rows
    while len(slots) < 2 + n_z:
        slots += list(range(small_rows, small_rows + TILE))
        small_rows += TILE
    small_rows = round_up(small_rows, TILE * n_rep)
    small_part = small_rows // n_rep
    rep_part = dense_part + small_part
    half = rep_part * n_rep
    tab_part = u_part + bag_part
    z_rows = rep_part + tab_part
    msg_rows = 3 * n_bag + TILE
    gb_rows = round_up(n_z, 8)

    def swap(value):
        return lax.ppermute(value, "core", [(0, 1), (1, 0)])

    def to_z(value, k):
        return lax.ppermute(value, "z", [(i, i ^ k) for i in range(n_z)])

    def to_rep(value, k):
        return lax.ppermute(value, "rep", [(i, i ^ k) for i in range(n_rep)])

    def spread(send, values, near_first=False):
        order = range(1, len(values))
        got = {k: send(values[k], k) for k in (order if near_first else reversed(order))}
        return [values[0]] + [got[k] for k in order]

    def call(body, out_shapes, args, name, scratch=()):
        return run(body, out_shapes, (spots, *args), name, scratch)

    spots = jnp.stack([lax.axis_index(name) for name in ("rep", "z", "core")]).astype(jnp.int32)
    spots = jnp.broadcast_to(jnp.pad(spots, (0, 5))[:, None], (8, 128))

    u_mine = lax.dynamic_slice_in_dim(u_emb, lax.axis_index("rep") * u_part, u_part, 0)
    u_z = spread(to_z, [u_mine] * n_z, True)[1:]

    def u_body(spot, *refs):
        for k, ref in enumerate(refs[:-1]):
            refs[-1][k * u_part : (k + 1) * u_part, :] = ref[...]

    (u_z,) = call(u_body, [shape((n_z - 1) * u_part, width)], u_z, "u_rows")
    u_r = spread(to_rep, [u_z] * n_rep)
    bias_rows = jnp.concatenate(
        [b[None].astype(F32) for b in (b_second, b_bot)] + [jnp.zeros((6, width), F32)]
    )

    def bags_body(spot, ct_ref, emb_ref, v_ref, b_ref, *outs):
        _, z, c = spot
        emb = emb_ref[...]
        emb_v = mul_nn(emb, v_ref[...]).astype(BF)
        bias = b_ref[...]
        for k, out in enumerate(outs):
            first = (z ^ k) * 2
            out[:n_bag, :own_rows] = ct_ref[:, cols_of(first + c, own_rows)].astype(F32).astype(BF)
            out[:n_bag, own_rows:] = (
                ct_ref[:, cols_of(first + 1 - c, own_rows)].astype(F32).astype(BF)
            )
            out[n_bag : 2 * n_bag, :] = emb
            out[2 * n_bag : 3 * n_bag, :] = emb_v
            out[3 * n_bag :, :] = bias

    counts_t = jnp.transpose(bag_counts, (1, 2, 0))[0]
    bags = call(
        bags_body,
        [shape(msg_rows, pair)] * n_z,
        (counts_t, emb_rows[0], v_emb, jnp.broadcast_to(b_emb[None], (TILE, width))),
        "bags",
    )
    bags = spread(to_z, bags, True)

    def cot_body(spot, cot_ref, out):
        _, _, c = spot
        for t in range(n_z):
            out[:, t * width : (t + 1) * width] = cot_ref[:, cols_of(2 * t + 1 - c, width)]

    (cot_out,) = call(cot_body, [shape(own_rows, n_z * width)], (cot_cross,), "cot_send")
    cot_in = swap(cot_out)

    feats_t = jnp.concatenate(
        [
            dense_feats.T,
            jnp.ones((1, own_rows), BF),
            jnp.zeros((feat_rows - n_feat - 1, own_rows), BF),
        ]
    )
    first_rows = jnp.concatenate(
        [w_first, b_first[None], jnp.zeros((feat_rows - n_feat - 1, hidden), BF)]
    )

    def mlp_body(
        spot, x_ref, w1_ref, w2_ref, b_ref, vb_ref, ub_ref, cot_ref,
        act_ref, slope1_ref, bottom_ref, slope2_ref, term_ref, back_ref,
    ):
        act, slope1_ref[...] = silu_parts(mul_tn(x_ref[...], w1_ref[...]))
        act = act.astype(BF)
        act_ref[...] = act
        bottom, slope2_ref[...] = silu_parts(mul_nn(act, w2_ref[...]) + b_ref[0:1, :])
        bottom = bottom.astype(BF)
        bottom_ref[...] = bottom
        term_ref[...] = mul_nn(bottom, vb_ref[...])
        d_lift = (cot_ref[...].astype(F32) * bottom.astype(F32)).astype(BF)
        back_ref[...] = mul_nt(d_lift, ub_ref[...])

    act, slope1, bottom, slope2, bot_term, bot_back = call(
        mlp_body,
        [
            shape(own_rows, hidden),
            shape(own_rows, hidden, F32),
            shape(own_rows, width),
            shape(own_rows, width, F32),
            shape(own_rows, width, F32),
            shape(own_rows, width, F32),
        ],
        (feats_t, first_rows, w_second, bias_rows, v_bot, u_bot, cot_bottom),
        "mlp_forward",
    )

    def part_body(spot, *refs):
        bag, u_refs = refs[:n_z], refs[n_z + 1 : n_z + 1 + n_rep]
        own_u, refs = refs[n_z], refs[n_z + 1 + n_rep :]
        cot_ref, cot_in_ref, term_ref, back_ref = refs[:4]
        part_ref, pooled_ref, lift_ref, u_ref, gb_ref = refs[4:]
        r, z, c = spot
        u_ref[:width, :] = own_u[...]
        for k in range(1, n_z):
            for j in range(n_rep):
                start = pl.multiple_of(k * width + (r ^ j) * u_part, TILE)
                u_ref[pl.ds(start, u_part), :] = u_refs[j][(k - 1) * u_part : k * u_part, :]
        low = jnp.zeros((pair, width), F32)
        back = jnp.zeros((pair, width), F32)
        gb_ref[...] = jnp.zeros_like(gb_ref)
        for k in range(n_z):
            rows = slice(k * width, (k + 1) * width)
            counts = bag[k][:n_bag, :]
            pooled = mul_tn(counts, bag[k][n_bag : 2 * n_bag, :]).astype(BF)
            low += mul_tn(counts, bag[k][2 * n_bag : 3 * n_bag, :])
            pooled_ref[rows, :] = pooled
            cot = jnp.concatenate(
                [cot_ref[:, cols_of(2 * (z ^ k) + c, width)], cot_in_ref[:, cols_of(z ^ k, width)]],
                axis=0,
            )
            d_lift = cot.astype(F32) * pooled.astype(F32)
            gb_ref[k : k + 1, :] = jnp.sum(d_lift, axis=0, keepdims=True) * grad_scale
            d_lift = d_lift.astype(BF)
            lift_ref[rows, :] = d_lift
            back += mul_nt(d_lift, u_ref[rows, :])
        part_ref[:own_rows, :] = (low[:own_rows] + term_ref[...]).astype(BF)
        part_ref[own_rows:pair, :] = low[own_rows:].astype(BF)
        part_ref[pair : pair + own_rows, :] = (back[:own_rows] + back_ref[...]).astype(BF)
        part_ref[pair + own_rows :, :] = back[own_rows:].astype(BF)

    part, pooled, d_lift, u_all, grad_b = call(
        part_body,
        [
            shape(2 * pair, width),
            shape(n_z * pair, width),
            shape(n_z * pair, width),
            shape(n_z * width, width),
            shape(gb_rows, width, F32),
        ],
        (*bags, u_emb, *u_r, cot_cross, cot_in, bot_term, bot_back),
        "partials",
    )
    part_in = swap(part)

    def summed(part_ref, in_ref, start):
        mid, end = start + own_rows, start + pair
        own = part_ref[start:mid, :].astype(F32) + in_ref[mid:end, :].astype(F32)
        other = part_ref[mid:end, :].astype(F32) + in_ref[start:mid, :].astype(F32)
        return own.astype(BF), other.astype(BF)

    def dense_body(
        spot, part_ref, in_ref, act_ref, slope1_ref, bottom_ref, slope2_ref, cot_ref, x_ref,
        w2_ref, vb_ref, ub_ref, b_ref, gb_ref,
        cross_ref, send_ref, keep_ref, pack, small,
    ):
        _, z, c = spot
        low, _ = summed(part_ref, in_ref, 0)
        d_low, _ = summed(part_ref, in_ref, pair)
        bottom = bottom_ref[...]
        bottom_full = bottom.astype(F32)
        cot = cot_ref[...].astype(F32)
        lift = mul_nn(low, ub_ref[...]) + b_ref[1:2, :] + 1.0
        cross_ref[...] = (bottom_full * lift).astype(BF)
        d_second = (cot * lift + mul_nt(d_low, vb_ref[...])) * slope2_ref[...]
        d_second_round = d_second.astype(BF)
        d_first = mul_nt(d_second_round, w2_ref[...]) * slope1_ref[...]
        d_bias = cot * bottom_full
        pack[...] = jnp.zeros_like(pack)

        def put(first, value):
            value = (value * grad_scale).astype(BF)
            at, last = first, first + value.shape[0]
            while at < last:
                block = at // dense_part
                end = min(last, (block + 1) * dense_part)
                start = block * rep_part + at - block * dense_part
                pack[start : start + end - at, :] = value[at - first : end - first]
                at = end

        put(0, mul_tn(act_ref[...], d_second_round))
        put(hidden, mul_tn(bottom, d_low))
        put(hidden + width, mul_tn(low, d_bias.astype(BF)))
        small[...] = jnp.zeros_like(small)
        g_first = mul_nn(x_ref[...], d_first.astype(BF)) * grad_scale
        for q in range(n_wide):
            small[q * feat_rows : (q + 1) * feat_rows, :] = g_first[
                :, q * width : (q + 1) * width
            ]
        small[slots[0] : slots[0] + 1, :] = jnp.sum(d_second, axis=0, keepdims=True) * grad_scale
        small[slots[1] : slots[1] + 1, :] = jnp.sum(d_bias, axis=0, keepdims=True) * grad_scale
        for slot in slots[2:]:
            small[slot : slot + 1, :] = jnp.zeros((1, width), F32)

        def put_small(which):
            for j in range(n_rep):
                start = pl.multiple_of((which * n_rep + j) * rep_part + dense_part, TILE)
                pack[pl.ds(start, small_part), :] = small[
                    j * small_part : (j + 1) * small_part, :
                ].astype(BF)

        put_small(1 - c)
        send_ref[...] = pack[rows_of(1 - c, half), :]
        for k in range(n_z):
            for t in range(n_z):

                @pl.when((z ^ k) == t)
                def _():
                    small[slots[2 + t] : slots[2 + t] + 1, :] = gb_ref[k : k + 1, :]

        put_small(c)
        keep_ref[...] = pack[rows_of(c, half), :]

    cross_bot, dense_out, dense_keep = call(
        dense_body,
        [shape(own_rows, width), shape(half, width), shape(half, width)],
        (
            part, part_in, act, slope1, bottom, slope2, cot_bottom, feats_t,
            w_second, v_bot, u_bot, bias_rows, grad_b,
        ),
        "dense_grads",
        [pltpu.VMEM((2 * half, width), BF), pltpu.VMEM((small_rows, width), F32)],
    )
    dense_in = swap(dense_out)

    def table_body(spot, *refs):
        bag = refs[:n_z]
        u_ref, part_ref, in_ref, pooled_ref, lift_ref, cot_ref, cot_in_ref = refs[n_z : n_z + 7]
        own_ref, send_ref, g_u, out = refs[n_z + 7 :]
        _, z, c = spot
        low = jnp.concatenate(summed(part_ref, in_ref, 0), axis=0)
        d_low = jnp.concatenate(summed(part_ref, in_ref, pair), axis=0)
        if bag_full > 2 * n_bag:
            out[...] = jnp.zeros_like(out)
        for k in range(n_z):
            base = k * width
            counts = bag[k][:n_bag, :]
            bias = bag[k][3 * n_bag :, :].astype(F32)[0:1]
            lift = mul_nn(low, u_ref[base : base + width, :]) + bias + 1.0
            cross = (pooled_ref[base : base + width, :].astype(F32) * lift).astype(BF)
            own_ref[:, cols_of(z ^ k, width)] = cross[:own_rows]
            send_ref[:, cols_of(z ^ k, width)] = cross[own_rows:]
            cot = jnp.concatenate(
                [cot_ref[:, cols_of(2 * (z ^ k) + c, width)], cot_in_ref[:, cols_of(z ^ k, width)]],
                axis=0,
            )
            direct = (cot.astype(F32) * lift).astype(BF)
            g_u[base : base + width, :] = (
                mul_tn(low, lift_ref[base : base + width, :]) * grad_scale
            ).astype(BF)
            start = k * bag_full
            out[start : start + n_bag, :] = (mul_nn(counts, d_low) * grad_scale).astype(BF)
            out[start + n_bag : start + 2 * n_bag, :] = (
                mul_nn(counts, direct) * grad_scale
            ).astype(BF)

    cross_own, cross_out, u_keep, bag_keep = call(
        table_body,
        [shape(own_rows, n_z * width)] * 2
        + [shape(n_z * width, width), shape(n_z * bag_full, width)],
        (*bags, u_all, part, part_in, pooled, d_lift, cot_cross, cot_in),
        "table_grads",
    )

    def pair_body(spot, keep_ref, in_ref, u_ref, bag_ref, *outs):
        r, _, _ = spot
        for j, out in enumerate(outs):
            rows = rows_of(r ^ j, rep_part)
            out[:rep_part, :] = (
                keep_ref[rows, :].astype(F32) + in_ref[rows, :].astype(F32)
            ).astype(BF)
            for k in range(n_z):
                start = rep_part + k * tab_part
                rows = pl.ds(pl.multiple_of(k * width + (r ^ j) * u_part, TILE), u_part)
                out[start : start + u_part, :] = u_ref[rows, :]
                rows = pl.ds(pl.multiple_of(k * bag_full + (r ^ j) * bag_part, TILE), bag_part)
                out[start + u_part : start + tab_part, :] = bag_ref[rows, :]

    rep_outs = call(
        pair_body,
        [shape(rep_part + n_z * tab_part, width)] * n_rep,
        (dense_keep, dense_in, u_keep, bag_keep),
        "pair_sum",
    )
    rep_ins = spread(to_rep, rep_outs)
    cross_in = swap(cross_out)

    def total(refs, first, count):
        return tree_sum([ref[first : first + count, :].astype(F32) for ref in refs]).astype(BF)

    def rep_body(spot, *refs):
        ins, outs = refs[:n_rep], refs[n_rep:]
        dense = total(ins, 0, rep_part)
        for k, out in enumerate(outs):
            out[:rep_part, :] = dense
            out[rep_part:, :] = total(ins, rep_part + k * tab_part, tab_part)

    z_outs = call(rep_body, [shape(z_rows, width)] * n_z, rep_ins, "rep_sum")
    z_ins = spread(to_z, z_outs, True)

    def cross_body(spot, own_ref, in_ref, out, done):
        _, _, c = spot
        done[...] = jnp.zeros_like(done)
        for t in range(n_z):
            cols = slice(t * width, (t + 1) * width)
            out[:, cols_of(2 * t + c, width)] = own_ref[:, cols]
            out[:, cols_of(2 * t + 1 - c, width)] = in_ref[:, cols]

    cross_emb, cross_done = call(
        cross_body,
        [shape(own_rows, 2 * n_z * width), shape(8, 128, F32)],
        (cross_own, cross_in),
        "cross_rows",
    )

    def z_body(spot, _, *refs):
        refs[n_z][...] = total(refs[:n_z], 0, z_rows)

    (mine,) = call(z_body, [shape(z_rows, width)], (cross_done, *z_ins), "z_sum")

    pieces = spread(to_rep, [mine] * n_rep)

    def gather_body(spot, *refs):
        r, _, _ = spot
        for j in range(n_rep):
            refs[n_rep][rows_of(r ^ j, dense_part), :] = refs[j][:dense_part, :]

    (dense_own,) = call(gather_body, [shape(n_rep * dense_part, width)], pieces, "dense_gather")
    dense_other = swap(dense_own)

    def table_last_body(spot, *refs):
        ins = refs[:n_rep]
        emb_ref, v_ref, g_table, g_v, g_u, g_wide, g_rows, stack, small = refs[n_rep:]
        r, z, _ = spot
        for j in range(n_rep):
            rows = slice(rep_part, rep_part + u_part)
            g_u[rows_of(r ^ j, u_part), :] = ins[j][rows, :]
            stack[rows_of(r ^ j, bag_part), :] = ins[j][rep_part + u_part :, :]
            small[rows_of(r ^ j, small_part), :] = ins[j][dense_part:rep_part, :].astype(F32)
        bag_low = stack[:n_bag, :]
        g_v[...] = mul_tn(emb_ref[...], bag_low).astype(BF)
        direct = stack[n_bag : 2 * n_bag, :].astype(F32)
        g_table[...] = (direct + mul_nt(bag_low, v_ref[...])).astype(BF)
        for q in range(n_wide):
            g_wide[:, q * width : (q + 1) * width] = small[q * feat_rows : (q + 1) * feat_rows, :]
        g_rows[...] = jnp.zeros_like(g_rows)
        for i in range(2):
            g_rows[i : i + 1, :] = small[slots[i] : slots[i] + 1, :]
        for t in range(n_z):

            @pl.when(z == t)
            def _():
                g_rows[2:3, :] = small[slots[2 + t] : slots[2 + t] + 1, :]

    grad_table, grad_v, grad_u, g_wide, g_rows = call(
        table_last_body,
        [
            shape(n_bag, width),
            shape(width, width),
            shape(width, width),
            shape(feat_rows, hidden, F32),
            shape(8, width, F32),
        ],
        (*pieces, emb_rows[0], v_emb),
        "table_last",
        [pltpu.VMEM((bag_full, width), BF), pltpu.VMEM((small_rows, width), F32)],
    )
    g_wide, g_rows = g_wide.astype(BF), g_rows.astype(BF)

    def dense_last_body(spot, own_ref, other_ref, g_second, g_vb, g_ub, stack):
        _, _, c = spot
        stack[rows_of(c, n_rep * dense_part), :] = own_ref[...]
        stack[rows_of(1 - c, n_rep * dense_part), :] = other_ref[...]
        g_second[...] = stack[:hidden, :]
        g_vb[...] = stack[hidden : hidden + width, :]
        g_ub[...] = stack[hidden + width : dense_rows, :]

    grad_ws, grad_vb, grad_ub = call(
        dense_last_body,
        [shape(hidden, width), shape(width, width), shape(width, width)],
        (dense_own, dense_other),
        "dense_last",
        [pltpu.VMEM((2 * n_rep * dense_part, width), BF)],
    )
    return (
        cross_emb,
        cross_bot,
        grad_table[None],
        grad_v,
        grad_u,
        g_rows[2],
        grad_vb,
        grad_ub,
        g_rows[1],
        g_wide[:n_feat],
        g_wide[n_feat],
        grad_ws,
        g_rows[0],
    )


def solution(mesh):
    n_rep, n_mp = mesh.devices.shape
    mesh = Mesh(mesh.devices.reshape(n_rep, n_mp // 2, 2), ("rep", "z", "core"))
    return jax.shard_map(
        local,
        mesh=mesh,
        in_specs=(
            P(("rep", "z", "core"), None),
            P("rep", ("z", "core"), None),
            P(("z", "core"), None, None),
            P(("z", "core"), None),
            P(None, ("z", "core")),
            P(("z", "core")),
            P(),
            P(),
            P(),
            P(),
            P(),
            P(),
            P(),
            P(("rep", "z", "core"), None),
            P(("rep", "z", "core"), None),
        ),
        out_specs=(
            P(("rep", "z", "core"), None),
            P(("rep", "z", "core"), None),
            P(("z", "core"), None, None),
            P(("z", "core"), None),
            P(None, ("z", "core")),
            P(("z", "core")),
            P(),
            P(),
            P(),
            P(),
            P(),
            P(),
            P(),
        ),
        check_vma=False,
    )
```

```python
import math

import jax
import jax.numpy as jnp
from jax import lax
from jax.experimental import pallas as pl
from jax.experimental.pallas import tpu as pltpu
from jax.sharding import Mesh
from jax.sharding import PartitionSpec as P

BF = jnp.bfloat16
F32 = jnp.float32
TILE = 16


def round_up(value, unit):
    return -(-value // unit) * unit


def silu_parts(inputs):
    gate_value = jax.nn.sigmoid(inputs)
    return inputs * gate_value, gate_value * (1.0 + inputs * (1.0 - gate_value))


def mul_nn(left, right):
    return lax.dot_general(left, right, (((1,), (0,)), ((), ())), preferred_element_type=F32)


def mul_tn(left, right):
    return lax.dot_general(left, right, (((0,), (0,)), ((), ())), preferred_element_type=F32)


def mul_nt(left, right):
    return lax.dot_general(left, right, (((1,), (1,)), ((), ())), preferred_element_type=F32)


def tree_sum(values):
    while len(values) > 1:
        values = [a + b for a, b in zip(values[::2], values[1::2])]
    return values[0]


def rows_of(index, count):
    return pl.ds(pl.multiple_of(index * count, TILE), count)


def cols_of(index, count):
    return pl.ds(pl.multiple_of(index * count, 128), count)


def run(body, out_shapes, args, name, scratch=(), flops=10**8, limit=6):
    in_vmem = pl.BlockSpec(memory_space=pltpu.VMEM)
    moved = sum(math.prod(a.shape) * a.dtype.itemsize for a in (*args, *out_shapes))

    def placed(spot_ref, *refs):
        body((spot_ref[0, 0], spot_ref[1, 0], spot_ref[2, 0]), *refs)

    return pl.pallas_call(
        placed,
        out_shape=out_shapes,
        in_specs=[in_vmem] * len(args),
        out_specs=[in_vmem] * len(out_shapes),
        scratch_shapes=list(scratch),
        compiler_params=pltpu.CompilerParams(vmem_limit_bytes=limit * 2**20),
        cost_estimate=pl.CostEstimate(flops=flops, bytes_accessed=moved, transcendentals=0),
        name=name,
    )(*args)


def shape(rows, cols, dtype=BF):
    return jax.ShapeDtypeStruct((rows, cols), dtype)


def local(
    dense_feats,
    bag_counts,
    emb_rows,
    v_emb,
    u_emb,
    b_emb,
    v_bot,
    u_bot,
    b_bot,
    w_first,
    b_first,
    w_second,
    b_second,
    cot_cross,
    cot_bottom,
):
    n_rep, n_z = lax.axis_size("rep"), lax.axis_size("z")
    own_rows, n_feat = dense_feats.shape
    hidden = w_first.shape[1]
    width = v_bot.shape[0]
    n_bag = bag_counts.shape[2]
    pair = 2 * own_rows
    grad_scale = 1.0 / math.sqrt(own_rows * 2 * n_z * n_rep)
    u_part = width // n_rep
    bag_part = round_up(-(-2 * n_bag // n_rep), TILE)
    bag_full = bag_part * n_rep
    dense_rows = hidden + 2 * width
    dense_part = round_up(-(-dense_rows // (2 * n_rep)), TILE)
    feat_rows = round_up(n_feat + 1, TILE)
    n_wide = hidden // width
    slots = [(q * feat_rows + i) for i in range(n_feat + 1, feat_rows) for q in range(n_wide)]
    small_rows = n_wide * feat_rows
    while len(slots) < 2 + n_z:
        slots += list(range(small_rows, small_rows + TILE))
        small_rows += TILE
    small_rows = round_up(small_rows, TILE * n_rep)
    small_part = small_rows // n_rep
    rep_part = dense_part + small_part
    half = rep_part * n_rep
    tab_part = u_part + bag_part
    z_rows = rep_part + tab_part
    msg_rows = 3 * n_bag + TILE
    gb_rows = round_up(n_z, 8)

    def swap(value):
        return lax.ppermute(value, "core", [(0, 1), (1, 0)])

    def to_z(value, k):
        return lax.ppermute(value, "z", [(i, i ^ k) for i in range(n_z)])

    def to_rep(value, k):
        return lax.ppermute(value, "rep", [(i, i ^ k) for i in range(n_rep)])

    def spread(send, values, near_first=False):
        order = range(1, len(values))
        got = {k: send(values[k], k) for k in (order if near_first else reversed(order))}
        return [values[0]] + [got[k] for k in order]

    def call(body, out_shapes, args, name, scratch=(), **options):
        return run(body, out_shapes, (spots, *args), name, scratch, **options)

    spots = jnp.stack([lax.axis_index(name) for name in ("rep", "z", "core")]).astype(jnp.int32)
    spots = jnp.broadcast_to(jnp.pad(spots, (0, 5))[:, None], (8, 128))

    def cut_body(spot, u_ref, out):
        out[...] = u_ref[rows_of(spot[0], u_part), :]

    (u_mine,) = call(cut_body, [shape(u_part, width)], (u_emb,), "u_cut", flops=2 * 10**10)
    u_z = spread(to_z, [u_mine] * n_z, True)[1:]

    def u_body(spot, *refs):
        for k, ref in enumerate(refs[:-1]):
            refs[-1][k * u_part : (k + 1) * u_part, :] = ref[...]

    (u_z,) = call(u_body, [shape((n_z - 1) * u_part, width)], u_z, "u_rows")
    u_r = spread(to_rep, [u_z] * n_rep)

    bias_rows = jnp.concatenate(
        [b[None].astype(F32) for b in (b_second, b_bot)] + [jnp.zeros((6, width), F32)]
    )

    def bags_body(spot, ct_ref, emb_ref, v_ref, b_ref, *outs):
        _, z, c = spot
        emb = emb_ref[...]
        emb_v = mul_nn(emb, v_ref[...]).astype(BF)
        bias = b_ref[...]
        for k, out in enumerate(outs):
            first = (z ^ k) * 2
            out[:n_bag, :own_rows] = ct_ref[:, cols_of(first + c, own_rows)].astype(F32).astype(BF)
            out[:n_bag, own_rows:] = (
                ct_ref[:, cols_of(first + 1 - c, own_rows)].astype(F32).astype(BF)
            )
            out[n_bag : 2 * n_bag, :] = emb
            out[2 * n_bag : 3 * n_bag, :] = emb_v
            out[3 * n_bag :, :] = bias

    counts_t = jnp.transpose(bag_counts, (1, 2, 0))[0]
    bags = call(
        bags_body,
        [shape(msg_rows, pair)] * n_z,
        (counts_t, emb_rows[0], v_emb, jnp.broadcast_to(b_emb[None], (TILE, width))),
        "bags",
    )
    bags = spread(to_z, bags, True)

    def cot_body(spot, cot_ref, out):
        _, _, c = spot
        for t in range(n_z):
            out[:, t * width : (t + 1) * width] = cot_ref[:, cols_of(2 * t + 1 - c, width)]

    (cot_out,) = call(cot_body, [shape(own_rows, n_z * width)], (cot_cross,), "cot_send")
    cot_in = swap(cot_out)

    feats_t = jnp.concatenate(
        [
            dense_feats.T,
            jnp.ones((1, own_rows), BF),
            jnp.zeros((feat_rows - n_feat - 1, own_rows), BF),
        ]
    )
    first_rows = jnp.concatenate(
        [w_first, b_first[None], jnp.zeros((feat_rows - n_feat - 1, hidden), BF)]
    )

    def mlp_body(
        spot, x_ref, w1_ref, w2_ref, b_ref, vb_ref, ub_ref, cot_ref,
        act_ref, slope1_ref, bottom_ref, slope2_ref, term_ref, back_ref,
    ):
        act, slope1_ref[...] = silu_parts(mul_tn(x_ref[...], w1_ref[...]))
        act = act.astype(BF)
        act_ref[...] = act
        bottom, slope2_ref[...] = silu_parts(mul_nn(act, w2_ref[...]) + b_ref[0:1, :])
        bottom = bottom.astype(BF)
        bottom_ref[...] = bottom
        term_ref[...] = mul_nn(bottom, vb_ref[...])
        d_lift = (cot_ref[...].astype(F32) * bottom.astype(F32)).astype(BF)
        back_ref[...] = mul_nt(d_lift, ub_ref[...])

    act, slope1, bottom, slope2, bot_term, bot_back = call(
        mlp_body,
        [
            shape(own_rows, hidden),
            shape(own_rows, hidden, F32),
            shape(own_rows, width),
            shape(own_rows, width, F32),
            shape(own_rows, width, F32),
            shape(own_rows, width, F32),
        ],
        (feats_t, first_rows, w_second, bias_rows, v_bot, u_bot, cot_bottom),
        "mlp_forward",
    )

    def part_body(spot, *refs):
        bag, u_refs = refs[:n_z], refs[n_z + 1 : n_z + 1 + n_rep]
        own_u, refs = refs[n_z], refs[n_z + 1 + n_rep :]
        cot_ref, cot_in_ref, term_ref, back_ref = refs[:4]
        part_ref, pooled_ref, lift_ref, u_ref, gb_ref = refs[4:]
        r, z, c = spot
        u_ref[:width, :] = own_u[...]
        for k in range(1, n_z):
            for j in range(n_rep):
                start = pl.multiple_of(k * width + (r ^ j) * u_part, TILE)
                u_ref[pl.ds(start, u_part), :] = u_refs[j][(k - 1) * u_part : k * u_part, :]
        low = jnp.zeros((pair, width), F32)
        back = jnp.zeros((pair, width), F32)
        gb_ref[...] = jnp.zeros_like(gb_ref)
        for k in range(n_z):
            rows = slice(k * width, (k + 1) * width)
            counts = bag[k][:n_bag, :]
            pooled = mul_tn(counts, bag[k][n_bag : 2 * n_bag, :]).astype(BF)
            low += mul_tn(counts, bag[k][2 * n_bag : 3 * n_bag, :])
            pooled_ref[rows, :] = pooled
            cot = jnp.concatenate(
                [cot_ref[:, cols_of(2 * (z ^ k) + c, width)], cot_in_ref[:, cols_of(z ^ k, width)]],
                axis=0,
            )
            d_lift = cot.astype(F32) * pooled.astype(F32)
            gb_ref[k : k + 1, :] = jnp.sum(d_lift, axis=0, keepdims=True) * grad_scale
            d_lift = d_lift.astype(BF)
            lift_ref[rows, :] = d_lift
            back += mul_nt(d_lift, u_ref[rows, :])
        part_ref[:own_rows, :] = (low[:own_rows] + term_ref[...]).astype(BF)
        part_ref[own_rows:pair, :] = low[own_rows:].astype(BF)
        part_ref[pair : pair + own_rows, :] = (back[:own_rows] + back_ref[...]).astype(BF)
        part_ref[pair + own_rows :, :] = back[own_rows:].astype(BF)

    part, pooled, d_lift, u_all, grad_b = call(
        part_body,
        [
            shape(2 * pair, width),
            shape(n_z * pair, width),
            shape(n_z * pair, width),
            shape(n_z * width, width),
            shape(gb_rows, width, F32),
        ],
        (*bags, u_emb, *u_r, cot_cross, cot_in, bot_term, bot_back),
        "partials",
    )
    part_in = swap(part)

    def summed(part_ref, in_ref, start):
        mid, end = start + own_rows, start + pair
        own = part_ref[start:mid, :].astype(F32) + in_ref[mid:end, :].astype(F32)
        other = part_ref[mid:end, :].astype(F32) + in_ref[start:mid, :].astype(F32)
        return own.astype(BF), other.astype(BF)

    def dense_body(
        spot, part_ref, in_ref, act_ref, slope1_ref, bottom_ref, slope2_ref, cot_ref, x_ref,
        w2_ref, vb_ref, ub_ref, b_ref, gb_ref,
        cross_ref, send_ref, keep_ref, pack, small,
    ):
        _, z, c = spot
        low, _ = summed(part_ref, in_ref, 0)
        d_low, _ = summed(part_ref, in_ref, pair)
        bottom = bottom_ref[...]
        bottom_full = bottom.astype(F32)
        cot = cot_ref[...].astype(F32)
        lift = mul_nn(low, ub_ref[...]) + b_ref[1:2, :] + 1.0
        cross_ref[...] = (bottom_full * lift).astype(BF)
        d_second = (cot * lift + mul_nt(d_low, vb_ref[...])) * slope2_ref[...]
        d_second_round = d_second.astype(BF)
        d_first = mul_nt(d_second_round, w2_ref[...]) * slope1_ref[...]
        d_bias = cot * bottom_full
        pack[...] = jnp.zeros_like(pack)

        def put(first, value):
            value = (value * grad_scale).astype(BF)
            at, last = first, first + value.shape[0]
            while at < last:
                block = at // dense_part
                end = min(last, (block + 1) * dense_part)
                start = block * rep_part + at - block * dense_part
                pack[start : start + end - at, :] = value[at - first : end - first]
                at = end

        put(0, mul_tn(act_ref[...], d_second_round))
        put(hidden, mul_tn(bottom, d_low))
        put(hidden + width, mul_tn(low, d_bias.astype(BF)))
        small[...] = jnp.zeros_like(small)
        g_first = mul_nn(x_ref[...], d_first.astype(BF)) * grad_scale
        for q in range(n_wide):
            small[q * feat_rows : (q + 1) * feat_rows, :] = g_first[
                :, q * width : (q + 1) * width
            ]
        small[slots[0] : slots[0] + 1, :] = jnp.sum(d_second, axis=0, keepdims=True) * grad_scale
        small[slots[1] : slots[1] + 1, :] = jnp.sum(d_bias, axis=0, keepdims=True) * grad_scale
        for slot in slots[2:]:
            small[slot : slot + 1, :] = jnp.zeros((1, width), F32)

        def put_small(which):
            for j in range(n_rep):
                start = pl.multiple_of((which * n_rep + j) * rep_part + dense_part, TILE)
                pack[pl.ds(start, small_part), :] = small[
                    j * small_part : (j + 1) * small_part, :
                ].astype(BF)

        put_small(1 - c)
        send_ref[...] = pack[rows_of(1 - c, half), :]
        for k in range(n_z):
            for t in range(n_z):

                @pl.when((z ^ k) == t)
                def _():
                    small[slots[2 + t] : slots[2 + t] + 1, :] = gb_ref[k : k + 1, :]

        put_small(c)
        keep_ref[...] = pack[rows_of(c, half), :]

    cross_bot, dense_out, dense_keep = call(
        dense_body,
        [shape(own_rows, width), shape(half, width), shape(half, width)],
        (
            part, part_in, act, slope1, bottom, slope2, cot_bottom, feats_t,
            w_second, v_bot, u_bot, bias_rows, grad_b,
        ),
        "dense_grads",
        [pltpu.VMEM((2 * half, width), BF), pltpu.VMEM((small_rows, width), F32)],
    )
    dense_in = swap(dense_out)

    def table_body(spot, *refs):
        bag = refs[:n_z]
        u_ref, part_ref, in_ref, pooled_ref, lift_ref, cot_ref, cot_in_ref = refs[n_z : n_z + 7]
        own_ref, send_ref, g_u, out = refs[n_z + 7 :]
        _, z, c = spot
        low = jnp.concatenate(summed(part_ref, in_ref, 0), axis=0)
        d_low = jnp.concatenate(summed(part_ref, in_ref, pair), axis=0)
        if bag_full > 2 * n_bag:
            out[...] = jnp.zeros_like(out)
        for k in range(n_z):
            base = k * width
            counts = bag[k][:n_bag, :]
            bias = bag[k][3 * n_bag :, :].astype(F32)[0:1]
            lift = mul_nn(low, u_ref[base : base + width, :]) + bias + 1.0
            cross = (pooled_ref[base : base + width, :].astype(F32) * lift).astype(BF)
            own_ref[:, cols_of(z ^ k, width)] = cross[:own_rows]
            send_ref[:, cols_of(z ^ k, width)] = cross[own_rows:]
            cot = jnp.concatenate(
                [cot_ref[:, cols_of(2 * (z ^ k) + c, width)], cot_in_ref[:, cols_of(z ^ k, width)]],
                axis=0,
            )
            direct = (cot.astype(F32) * lift).astype(BF)
            g_u[base : base + width, :] = (
                mul_tn(low, lift_ref[base : base + width, :]) * grad_scale
            ).astype(BF)
            start = k * bag_full
            out[start : start + n_bag, :] = (mul_nn(counts, d_low) * grad_scale).astype(BF)
            out[start + n_bag : start + 2 * n_bag, :] = (
                mul_nn(counts, direct) * grad_scale
            ).astype(BF)

    cross_own, cross_out, u_keep, bag_keep = call(
        table_body,
        [shape(own_rows, n_z * width)] * 2
        + [shape(n_z * width, width), shape(n_z * bag_full, width)],
        (*bags, u_all, part, part_in, pooled, d_lift, cot_cross, cot_in),
        "table_grads",
    )

    rep_rows = rep_part + n_z * tab_part
    cut = round_up(rep_rows // 2, TILE) - TILE if n_rep == 4 else rep_rows
    if n_rep == 4:
        homes = {
            (0, 0): (0, 0), (2, 0): (0, cut), (1, 0): (1, 0), (3, 0): (1, cut),
            (0, 1): (2, 0), (1, 1): (2, rep_rows - cut), (2, 1): (3, 0), (3, 1): (3, rep_rows - cut),
        }
        pair_shapes = [shape(2 * cut, width)] * 2 + [shape(2 * (rep_rows - cut), width)] * 2
    else:
        homes = {(j, 0): (j, 0) for j in range(n_rep)}
        pair_shapes = [shape(rep_rows, width)] * n_rep

    def pair_body(spot, keep_ref, in_ref, u_ref, bag_ref, *outs):
        r, _, _ = spot

        def put(j, first, value):
            last = first + value.shape[0]
            for part, (low, high) in enumerate(((0, cut), (cut, rep_rows))):
                start, end = max(first, low), min(last, high)
                if start < end:
                    which, base = homes[j, part]
                    outs[which][base + start - low : base + end - low, :] = value[
                        start - first : end - first
                    ]

        for j in range(n_rep):
            rows = rows_of(r ^ j, rep_part)
            put(j, 0, (keep_ref[rows, :].astype(F32) + in_ref[rows, :].astype(F32)).astype(BF))
            for k in range(n_z):
                start = rep_part + k * tab_part
                rows = pl.ds(pl.multiple_of(k * width + (r ^ j) * u_part, TILE), u_part)
                put(j, start, u_ref[rows, :])
                rows = pl.ds(pl.multiple_of(k * bag_full + (r ^ j) * bag_part, TILE), bag_part)
                put(j, start + u_part, bag_ref[rows, :])

    outs = call(pair_body, pair_shapes, (dense_keep, dense_in, u_keep, bag_keep), "pair_sum")

    def total(refs, first, count):
        return tree_sum([ref[first : first + count, :].astype(F32) for ref in refs]).astype(BF)

    if n_rep == 4:
        one_in, two_in = to_rep(outs[1], 1), to_rep(outs[3], 2)

        def half_body(spot, one_ref, one_in_ref, two_ref, two_in_ref, keep, one_out, two_out):
            rest = rep_rows - cut
            keep[:cut, :] = total((one_ref, one_in_ref), 0, cut)
            one_out[...] = total((one_ref, one_in_ref), cut, cut)
            keep[cut:, :] = total((two_ref, two_in_ref), 0, rest)
            two_out[...] = total((two_ref, two_in_ref), rest, rest)

        keep, one_out, two_out = call(
            half_body,
            [shape(rep_rows, width), shape(cut, width), shape(rep_rows - cut, width)],
            (outs[0], one_in, outs[2], two_in),
            "half_sum",
        )
        rep_ins = [keep, to_rep(one_out, 2), to_rep(two_out, 1)]
    else:
        rep_ins = spread(to_rep, outs)
    cross_in = swap(cross_out)

    def rep_body(spot, *refs):
        ins, outs = refs[: len(rep_ins)], refs[len(rep_ins) :]

        def rows_sum(first, count):
            if n_rep != 4:
                return [total(ins, first, count)]
            parts = []
            if first < cut:
                parts.append(total(ins[:2], first, min(count, cut - first)))
            if first + count > cut:
                start, end = max(first, cut), first + count
                kept = ins[0][start:end, :].astype(F32)
                parts.append((kept + ins[2][start - cut : end - cut, :].astype(F32)).astype(BF))
            return parts

        def put(out, at, parts):
            for value in parts:
                out[at : at + value.shape[0], :] = value
                at += value.shape[0]

        dense = rows_sum(0, rep_part)
        for k, out in enumerate(outs):
            put(out, 0, dense)
            put(out, rep_part, rows_sum(rep_part + k * tab_part, tab_part))

    z_outs = call(rep_body, [shape(z_rows, width)] * n_z, rep_ins, "rep_sum")
    z_ins = spread(to_z, z_outs, True)

    def cross_body(spot, own_ref, in_ref, out, done):
        _, _, c = spot
        done[...] = jnp.zeros_like(done)
        for t in range(n_z):
            cols = slice(t * width, (t + 1) * width)
            out[:, cols_of(2 * t + c, width)] = own_ref[:, cols]
            out[:, cols_of(2 * t + 1 - c, width)] = in_ref[:, cols]

    cross_emb, cross_done = call(
        cross_body,
        [shape(own_rows, 2 * n_z * width), shape(8, 128, F32)],
        (cross_own, cross_in),
        "cross_rows",
    )

    def z_body(spot, _, *refs):
        refs[n_z][...] = total(refs[:n_z], 0, z_rows)

    (mine,) = call(z_body, [shape(z_rows, width)], (cross_done, *z_ins), "z_sum")

    pieces = spread(to_rep, [mine] * n_rep)

    def gather_body(spot, *refs):
        r, _, _ = spot
        for j in range(n_rep):
            refs[n_rep][rows_of(r ^ j, dense_part), :] = refs[j][:dense_part, :]

    (dense_own,) = call(gather_body, [shape(n_rep * dense_part, width)], pieces, "dense_gather")
    dense_other = swap(dense_own)

    def table_last_body(spot, *refs):
        ins = refs[:n_rep]
        emb_ref, v_ref, g_table, g_v, g_u, g_wide, g_rows, stack, small = refs[n_rep:]
        r, z, _ = spot
        for j in range(n_rep):
            rows = slice(rep_part, rep_part + u_part)
            g_u[rows_of(r ^ j, u_part), :] = ins[j][rows, :]
            stack[rows_of(r ^ j, bag_part), :] = ins[j][rep_part + u_part :, :]
            small[rows_of(r ^ j, small_part), :] = ins[j][dense_part:rep_part, :].astype(F32)
        bag_low = stack[:n_bag, :]
        g_v[...] = mul_tn(emb_ref[...], bag_low).astype(BF)
        direct = stack[n_bag : 2 * n_bag, :].astype(F32)
        g_table[...] = (direct + mul_nt(bag_low, v_ref[...])).astype(BF)
        for q in range(n_wide):
            g_wide[:, q * width : (q + 1) * width] = small[q * feat_rows : (q + 1) * feat_rows, :]
        g_rows[...] = jnp.zeros_like(g_rows)
        for i in range(2):
            g_rows[i : i + 1, :] = small[slots[i] : slots[i] + 1, :]
        for t in range(n_z):

            @pl.when(z == t)
            def _():
                g_rows[2:3, :] = small[slots[2 + t] : slots[2 + t] + 1, :]

    grad_table, grad_v, grad_u, g_wide, g_rows = call(
        table_last_body,
        [
            shape(n_bag, width),
            shape(width, width),
            shape(width, width),
            shape(feat_rows, hidden, F32),
            shape(8, width, F32),
        ],
        (*pieces, emb_rows[0], v_emb),
        "table_last",
        [pltpu.VMEM((bag_full, width), BF), pltpu.VMEM((small_rows, width), F32)],
    )
    g_wide, g_rows = g_wide.astype(BF), g_rows.astype(BF)

    def dense_last_body(spot, own_ref, other_ref, g_second, g_vb, g_ub, stack):
        _, _, c = spot
        stack[rows_of(c, n_rep * dense_part), :] = own_ref[...]
        stack[rows_of(1 - c, n_rep * dense_part), :] = other_ref[...]
        g_second[...] = stack[:hidden, :]
        g_vb[...] = stack[hidden : hidden + width, :]
        g_ub[...] = stack[hidden + width : dense_rows, :]

    grad_ws, grad_vb, grad_ub = call(
        dense_last_body,
        [shape(hidden, width), shape(width, width), shape(width, width)],
        (dense_own, dense_other),
        "dense_last",
        [pltpu.VMEM((2 * n_rep * dense_part, width), BF)],
    )
    return (
        cross_emb,
        cross_bot,
        grad_table[None],
        grad_v,
        grad_u,
        g_rows[2],
        grad_vb,
        grad_ub,
        g_rows[1],
        g_wide[:n_feat],
        g_wide[n_feat],
        grad_ws,
        g_rows[0],
    )


def solution(mesh):
    n_rep, n_mp = mesh.devices.shape
    mesh = Mesh(mesh.devices.reshape(n_rep, n_mp // 2, 2), ("rep", "z", "core"))
    return jax.shard_map(
        local,
        mesh=mesh,
        in_specs=(
            P(("rep", "z", "core"), None),
            P("rep", ("z", "core"), None),
            P(("z", "core"), None, None),
            P(("z", "core"), None),
            P(None, ("z", "core")),
            P(("z", "core")),
            P(),
            P(),
            P(),
            P(),
            P(),
            P(),
            P(),
            P(("rep", "z", "core"), None),
            P(("rep", "z", "core"), None),
        ),
        out_specs=(
            P(("rep", "z", "core"), None),
            P(("rep", "z", "core"), None),
            P(("z", "core"), None, None),
            P(("z", "core"), None),
            P(None, ("z", "core")),
            P(("z", "core")),
            P(),
            P(),
            P(),
            P(),
            P(),
            P(),
            P(),
        ),
        check_vma=False,
    )
```

```python
import math

import jax
import jax.numpy as jnp
from jax import lax
from jax.experimental import pallas as pl
from jax.experimental.pallas import tpu as pltpu
from jax.sharding import Mesh
from jax.sharding import PartitionSpec as P

BF = jnp.bfloat16
F32 = jnp.float32
TILE = 16


def round_up(value, unit):
    return -(-value // unit) * unit


def silu_parts(inputs):
    gate_value = jax.nn.sigmoid(inputs)
    return inputs * gate_value, gate_value * (1.0 + inputs * (1.0 - gate_value))


def mul_nn(left, right):
    return lax.dot_general(left, right, (((1,), (0,)), ((), ())), preferred_element_type=F32)


def mul_tn(left, right):
    return lax.dot_general(left, right, (((0,), (0,)), ((), ())), preferred_element_type=F32)


def mul_nt(left, right):
    return lax.dot_general(left, right, (((1,), (1,)), ((), ())), preferred_element_type=F32)


def tree_sum(values):
    while len(values) > 1:
        values = [a + b for a, b in zip(values[::2], values[1::2])]
    return values[0]


def rows_of(index, count):
    return pl.ds(pl.multiple_of(index * count, TILE), count)


def cols_of(index, count):
    return pl.ds(pl.multiple_of(index * count, 128), count)


def run(body, out_shapes, args, name, scratch=(), flops=10**8, limit=6):
    in_vmem = pl.BlockSpec(memory_space=pltpu.VMEM)
    moved = sum(math.prod(a.shape) * a.dtype.itemsize for a in (*args, *out_shapes))

    def placed(spot_ref, *refs):
        body((spot_ref[0, 0], spot_ref[1, 0], spot_ref[2, 0]), *refs)

    return pl.pallas_call(
        placed,
        out_shape=out_shapes,
        in_specs=[in_vmem] * len(args),
        out_specs=[in_vmem] * len(out_shapes),
        scratch_shapes=list(scratch),
        compiler_params=pltpu.CompilerParams(vmem_limit_bytes=limit * 2**20),
        cost_estimate=pl.CostEstimate(flops=flops, bytes_accessed=moved, transcendentals=0),
        name=name,
    )(*args)


def shape(rows, cols, dtype=BF):
    return jax.ShapeDtypeStruct((rows, cols), dtype)


def local(
    dense_feats,
    bag_counts,
    emb_rows,
    v_emb,
    u_emb,
    b_emb,
    v_bot,
    u_bot,
    b_bot,
    w_first,
    b_first,
    w_second,
    b_second,
    cot_cross,
    cot_bottom,
):
    n_rep, n_z = lax.axis_size("rep"), lax.axis_size("z")
    own_rows, n_feat = dense_feats.shape
    hidden = w_first.shape[1]
    width = v_bot.shape[0]
    n_bag = bag_counts.shape[2]
    pair = 2 * own_rows
    grad_scale = 1.0 / math.sqrt(own_rows * 2 * n_z * n_rep)
    u_part = width // n_rep
    bag_part = round_up(-(-2 * n_bag // n_rep), TILE)
    bag_full = bag_part * n_rep
    dense_rows = hidden + 2 * width
    dense_part = round_up(-(-dense_rows // (2 * n_rep)), TILE)
    feat_rows = round_up(n_feat + 1, TILE)
    n_wide = hidden // width
    slots = [(q * feat_rows + i) for i in range(n_feat + 1, feat_rows) for q in range(n_wide)]
    small_rows = n_wide * feat_rows
    while len(slots) < 2 + n_z:
        slots += list(range(small_rows, small_rows + TILE))
        small_rows += TILE
    small_rows = round_up(small_rows, TILE * n_rep)
    small_part = small_rows // n_rep
    rep_part = dense_part + small_part
    half = rep_part * n_rep
    tab_part = u_part + bag_part
    z_rows = rep_part + tab_part
    msg_rows = 3 * n_bag + TILE
    gb_rows = round_up(n_z, 8)

    def swap(value):
        return lax.ppermute(value, "core", [(0, 1), (1, 0)])

    def to_z(value, k):
        return lax.ppermute(value, "z", [(i, i ^ k) for i in range(n_z)])

    def to_rep(value, k):
        return lax.ppermute(value, "rep", [(i, i ^ k) for i in range(n_rep)])

    def spread(send, values, near_first=False):
        order = range(1, len(values))
        got = {k: send(values[k], k) for k in (order if near_first else reversed(order))}
        return [values[0]] + [got[k] for k in order]

    def call(body, out_shapes, args, name, scratch=(), **options):
        return run(body, out_shapes, (spots, *args), name, scratch, **options)

    spots = jnp.stack([lax.axis_index(name) for name in ("rep", "z", "core")]).astype(jnp.int32)
    spots = jnp.broadcast_to(jnp.pad(spots, (0, 5))[:, None], (8, 128))

    def cut_body(spot, u_ref, out):
        out[...] = u_ref[rows_of(spot[0], u_part), :]

    (u_mine,) = call(cut_body, [shape(u_part, width)], (u_emb,), "u_cut", flops=2 * 10**10)
    u_z = spread(to_z, [u_mine] * n_z, True)[1:]

    def u_body(spot, *refs):
        for k, ref in enumerate(refs[:-1]):
            refs[-1][k * u_part : (k + 1) * u_part, :] = ref[...]

    (u_z,) = call(u_body, [shape((n_z - 1) * u_part, width)], u_z, "u_rows")
    u_r = spread(to_rep, [u_z] * n_rep)

    bias_rows = jnp.concatenate(
        [b[None].astype(F32) for b in (b_second, b_bot)] + [jnp.zeros((6, width), F32)]
    )

    def bags_body(spot, ct_ref, emb_ref, v_ref, b_ref, *outs):
        _, z, c = spot
        emb = emb_ref[...]
        emb_v = mul_nn(emb, v_ref[...]).astype(BF)
        bias = b_ref[...]
        for k, out in enumerate(outs):
            first = (z ^ k) * 2
            out[:n_bag, :own_rows] = ct_ref[:, cols_of(first + c, own_rows)].astype(F32).astype(BF)
            out[:n_bag, own_rows:] = (
                ct_ref[:, cols_of(first + 1 - c, own_rows)].astype(F32).astype(BF)
            )
            out[n_bag : 2 * n_bag, :] = emb
            out[2 * n_bag : 3 * n_bag, :] = emb_v
            out[3 * n_bag :, :] = bias

    counts_t = jnp.transpose(bag_counts, (1, 2, 0))[0]
    bags = call(
        bags_body,
        [shape(msg_rows, pair)] * n_z,
        (counts_t, emb_rows[0], v_emb, jnp.broadcast_to(b_emb[None], (TILE, width))),
        "bags",
    )
    bags = spread(to_z, bags, True)

    def cot_body(spot, cot_ref, out):
        _, _, c = spot
        for t in range(n_z):
            out[:, t * width : (t + 1) * width] = cot_ref[:, cols_of(2 * t + 1 - c, width)]

    (cot_out,) = call(cot_body, [shape(own_rows, n_z * width)], (cot_cross,), "cot_send")
    cot_in = swap(cot_out)

    feats_t = jnp.concatenate(
        [
            dense_feats.T,
            jnp.ones((1, own_rows), BF),
            jnp.zeros((feat_rows - n_feat - 1, own_rows), BF),
        ]
    )
    first_rows = jnp.concatenate(
        [w_first, b_first[None], jnp.zeros((feat_rows - n_feat - 1, hidden), BF)]
    )

    def mlp_body(
        spot, x_ref, w1_ref, w2_ref, b_ref, vb_ref, ub_ref, cot_ref,
        act_ref, slope1_ref, bottom_ref, slope2_ref, term_ref, back_ref,
    ):
        act, slope1_ref[...] = silu_parts(mul_tn(x_ref[...], w1_ref[...]))
        act = act.astype(BF)
        act_ref[...] = act
        bottom, slope2_ref[...] = silu_parts(mul_nn(act, w2_ref[...]) + b_ref[0:1, :])
        bottom = bottom.astype(BF)
        bottom_ref[...] = bottom
        term_ref[...] = mul_nn(bottom, vb_ref[...])
        d_lift = (cot_ref[...].astype(F32) * bottom.astype(F32)).astype(BF)
        back_ref[...] = mul_nt(d_lift, ub_ref[...])

    act, slope1, bottom, slope2, bot_term, bot_back = call(
        mlp_body,
        [
            shape(own_rows, hidden),
            shape(own_rows, hidden, F32),
            shape(own_rows, width),
            shape(own_rows, width, F32),
            shape(own_rows, width, F32),
            shape(own_rows, width, F32),
        ],
        (feats_t, first_rows, w_second, bias_rows, v_bot, u_bot, cot_bottom),
        "mlp_forward",
    )

    def part_body(spot, *refs):
        bag, u_refs = refs[:n_z], refs[n_z + 1 : n_z + 1 + n_rep]
        own_u, refs = refs[n_z], refs[n_z + 1 + n_rep :]
        cot_ref, cot_in_ref, term_ref, back_ref = refs[:4]
        part_ref, pooled_ref, lift_ref, u_ref, gb_ref = refs[4:]
        r, z, c = spot
        u_ref[:width, :] = own_u[...]
        for k in range(1, n_z):
            for j in range(n_rep):
                start = pl.multiple_of(k * width + (r ^ j) * u_part, TILE)
                u_ref[pl.ds(start, u_part), :] = u_refs[j][(k - 1) * u_part : k * u_part, :]
        low = jnp.zeros((pair, width), F32)
        back = jnp.zeros((pair, width), F32)
        gb_ref[...] = jnp.zeros_like(gb_ref)
        for k in range(n_z):
            rows = slice(k * width, (k + 1) * width)
            counts = bag[k][:n_bag, :]
            pooled = mul_tn(counts, bag[k][n_bag : 2 * n_bag, :]).astype(BF)
            low += mul_tn(counts, bag[k][2 * n_bag : 3 * n_bag, :])
            pooled_ref[rows, :] = pooled
            cot = jnp.concatenate(
                [cot_ref[:, cols_of(2 * (z ^ k) + c, width)], cot_in_ref[:, cols_of(z ^ k, width)]],
                axis=0,
            )
            d_lift = cot.astype(F32) * pooled.astype(F32)
            gb_ref[k : k + 1, :] = jnp.sum(d_lift, axis=0, keepdims=True) * grad_scale
            d_lift = d_lift.astype(BF)
            lift_ref[rows, :] = d_lift
            back += mul_nt(d_lift, u_ref[rows, :])
        part_ref[:own_rows, :] = (low[:own_rows] + term_ref[...]).astype(BF)
        part_ref[own_rows:pair, :] = low[own_rows:].astype(BF)
        part_ref[pair : pair + own_rows, :] = (back[:own_rows] + back_ref[...]).astype(BF)
        part_ref[pair + own_rows :, :] = back[own_rows:].astype(BF)

    part, pooled, d_lift, u_all, grad_b = call(
        part_body,
        [
            shape(2 * pair, width),
            shape(n_z * pair, width),
            shape(n_z * pair, width),
            shape(n_z * width, width),
            shape(gb_rows, width, F32),
        ],
        (*bags, u_emb, *u_r, cot_cross, cot_in, bot_term, bot_back),
        "partials",
    )
    part_in = swap(part)

    def summed(part_ref, in_ref, start):
        mid, end = start + own_rows, start + pair
        own = part_ref[start:mid, :].astype(F32) + in_ref[mid:end, :].astype(F32)
        other = part_ref[mid:end, :].astype(F32) + in_ref[start:mid, :].astype(F32)
        return own.astype(BF), other.astype(BF)

    def dense_body(
        spot, part_ref, in_ref, act_ref, slope1_ref, bottom_ref, slope2_ref, cot_ref, x_ref,
        w2_ref, vb_ref, ub_ref, b_ref, gb_ref,
        cross_ref, send_ref, keep_ref, pack, small,
    ):
        _, z, c = spot
        low, _ = summed(part_ref, in_ref, 0)
        d_low, _ = summed(part_ref, in_ref, pair)
        bottom = bottom_ref[...]
        bottom_full = bottom.astype(F32)
        cot = cot_ref[...].astype(F32)
        lift = mul_nn(low, ub_ref[...]) + b_ref[1:2, :] + 1.0
        cross_ref[...] = (bottom_full * lift).astype(BF)
        d_second = (cot * lift + mul_nt(d_low, vb_ref[...])) * slope2_ref[...]
        d_second_round = d_second.astype(BF)
        d_first = mul_nt(d_second_round, w2_ref[...]) * slope1_ref[...]
        d_bias = cot * bottom_full
        pack[...] = jnp.zeros_like(pack)

        def put(first, value):
            value = (value * grad_scale).astype(BF)
            at, last = first, first + value.shape[0]
            while at < last:
                block = at // dense_part
                end = min(last, (block + 1) * dense_part)
                start = block * rep_part + at - block * dense_part
                pack[start : start + end - at, :] = value[at - first : end - first]
                at = end

        put(0, mul_tn(act_ref[...], d_second_round))
        put(hidden, mul_tn(bottom, d_low))
        put(hidden + width, mul_tn(low, d_bias.astype(BF)))
        small[...] = jnp.zeros_like(small)
        g_first = mul_nn(x_ref[...], d_first.astype(BF)) * grad_scale
        for q in range(n_wide):
            small[q * feat_rows : (q + 1) * feat_rows, :] = g_first[
                :, q * width : (q + 1) * width
            ]
        small[slots[0] : slots[0] + 1, :] = jnp.sum(d_second, axis=0, keepdims=True) * grad_scale
        small[slots[1] : slots[1] + 1, :] = jnp.sum(d_bias, axis=0, keepdims=True) * grad_scale
        for slot in slots[2:]:
            small[slot : slot + 1, :] = jnp.zeros((1, width), F32)

        def put_small(which):
            for j in range(n_rep):
                start = pl.multiple_of((which * n_rep + j) * rep_part + dense_part, TILE)
                pack[pl.ds(start, small_part), :] = small[
                    j * small_part : (j + 1) * small_part, :
                ].astype(BF)

        put_small(1 - c)
        send_ref[...] = pack[rows_of(1 - c, half), :]
        for k in range(n_z):
            for t in range(n_z):

                @pl.when((z ^ k) == t)
                def _():
                    small[slots[2 + t] : slots[2 + t] + 1, :] = gb_ref[k : k + 1, :]

        put_small(c)
        keep_ref[...] = pack[rows_of(c, half), :]

    cross_bot, dense_out, dense_keep = call(
        dense_body,
        [shape(own_rows, width), shape(half, width), shape(half, width)],
        (
            part, part_in, act, slope1, bottom, slope2, cot_bottom, feats_t,
            w_second, v_bot, u_bot, bias_rows, grad_b,
        ),
        "dense_grads",
        [pltpu.VMEM((2 * half, width), BF), pltpu.VMEM((small_rows, width), F32)],
    )
    dense_in = swap(dense_out)

    def table_body(spot, *refs):
        bag = refs[:n_z]
        u_ref, part_ref, in_ref, pooled_ref, lift_ref, cot_ref, cot_in_ref = refs[n_z : n_z + 7]
        own_ref, send_ref, g_u, out = refs[n_z + 7 :]
        _, z, c = spot
        low = jnp.concatenate(summed(part_ref, in_ref, 0), axis=0)
        d_low = jnp.concatenate(summed(part_ref, in_ref, pair), axis=0)
        if bag_full > 2 * n_bag:
            out[...] = jnp.zeros_like(out)
        for k in range(n_z):
            base = k * width
            counts = bag[k][:n_bag, :]
            bias = bag[k][3 * n_bag :, :].astype(F32)[0:1]
            lift = mul_nn(low, u_ref[base : base + width, :]) + bias + 1.0
            cross = (pooled_ref[base : base + width, :].astype(F32) * lift).astype(BF)
            own_ref[:, cols_of(z ^ k, width)] = cross[:own_rows]
            send_ref[:, cols_of(z ^ k, width)] = cross[own_rows:]
            cot = jnp.concatenate(
                [cot_ref[:, cols_of(2 * (z ^ k) + c, width)], cot_in_ref[:, cols_of(z ^ k, width)]],
                axis=0,
            )
            direct = (cot.astype(F32) * lift).astype(BF)
            g_u[base : base + width, :] = (
                mul_tn(low, lift_ref[base : base + width, :]) * grad_scale
            ).astype(BF)
            start = k * bag_full
            out[start : start + n_bag, :] = (mul_nn(counts, d_low) * grad_scale).astype(BF)
            out[start + n_bag : start + 2 * n_bag, :] = (
                mul_nn(counts, direct) * grad_scale
            ).astype(BF)

    cross_own, cross_out, u_keep, bag_keep = call(
        table_body,
        [shape(own_rows, n_z * width)] * 2
        + [shape(n_z * width, width), shape(n_z * bag_full, width)],
        (*bags, u_all, part, part_in, pooled, d_lift, cot_cross, cot_in),
        "table_grads",
    )

    rep_rows = rep_part + n_z * tab_part
    cut = round_up(rep_rows // 2, TILE) - TILE if n_rep == 4 else rep_rows
    if n_rep == 4:
        homes = {
            (0, 0): (0, 0), (2, 0): (0, cut), (1, 0): (1, 0), (3, 0): (1, cut),
            (0, 1): (2, 0), (1, 1): (2, rep_rows - cut), (2, 1): (3, 0), (3, 1): (3, rep_rows - cut),
        }
        pair_shapes = [shape(2 * cut, width)] * 2 + [shape(2 * (rep_rows - cut), width)] * 2
    else:
        homes = {(j, 0): (j, 0) for j in range(n_rep)}
        pair_shapes = [shape(rep_rows, width)] * n_rep

    def pair_body(spot, keep_ref, in_ref, u_ref, bag_ref, *outs):
        r, _, _ = spot

        def put(j, first, value):
            last = first + value.shape[0]
            for part, (low, high) in enumerate(((0, cut), (cut, rep_rows))):
                start, end = max(first, low), min(last, high)
                if start < end:
                    which, base = homes[j, part]
                    outs[which][base + start - low : base + end - low, :] = value[
                        start - first : end - first
                    ]

        for j in range(n_rep):
            rows = rows_of(r ^ j, rep_part)
            put(j, 0, (keep_ref[rows, :].astype(F32) + in_ref[rows, :].astype(F32)).astype(BF))
            for k in range(n_z):
                start = rep_part + k * tab_part
                rows = pl.ds(pl.multiple_of(k * width + (r ^ j) * u_part, TILE), u_part)
                put(j, start, u_ref[rows, :])
                rows = pl.ds(pl.multiple_of(k * bag_full + (r ^ j) * bag_part, TILE), bag_part)
                put(j, start + u_part, bag_ref[rows, :])

    outs = call(pair_body, pair_shapes, (dense_keep, dense_in, u_keep, bag_keep), "pair_sum")

    def total(refs, first, count):
        return tree_sum([ref[first : first + count, :].astype(F32) for ref in refs]).astype(BF)

    if n_rep == 4:
        one_in, two_in = to_rep(outs[1], 1), to_rep(outs[3], 2)

        def half_body(spot, one_ref, one_in_ref, two_ref, two_in_ref, keep, one_out, two_out):
            rest = rep_rows - cut
            keep[:cut, :] = total((one_ref, one_in_ref), 0, cut)
            one_out[...] = total((one_ref, one_in_ref), cut, cut)
            keep[cut:, :] = total((two_ref, two_in_ref), 0, rest)
            two_out[...] = total((two_ref, two_in_ref), rest, rest)

        keep, one_out, two_out = call(
            half_body,
            [shape(rep_rows, width), shape(cut, width), shape(rep_rows - cut, width)],
            (outs[0], one_in, outs[2], two_in),
            "half_sum",
        )
        rep_ins = [keep, to_rep(one_out, 2), to_rep(two_out, 1)]
    else:
        rep_ins = spread(to_rep, outs)
    cross_in = swap(cross_out)

    def rep_body(spot, *refs):
        ins, outs = refs[: len(rep_ins)], refs[len(rep_ins) :]

        def rows_sum(first, count):
            if n_rep != 4:
                return [total(ins, first, count)]
            parts = []
            if first < cut:
                parts.append(total(ins[:2], first, min(count, cut - first)))
            if first + count > cut:
                start, end = max(first, cut), first + count
                kept = ins[0][start:end, :].astype(F32)
                parts.append((kept + ins[2][start - cut : end - cut, :].astype(F32)).astype(BF))
            return parts

        def put(out, at, parts):
            for value in parts:
                out[at : at + value.shape[0], :] = value
                at += value.shape[0]

        dense = rows_sum(0, rep_part)
        for i, out in enumerate(outs):
            put(out, 0, dense)
            for n, k in enumerate(trips[i]):
                put(out, rep_part + n * tab_part, rows_sum(rep_part + k * tab_part, tab_part))

    trips = [(0, 2), (1, 3)] if n_z == 4 else [(k,) for k in range(n_z)]
    z_outs = call(
        rep_body,
        [shape(rep_part + len(trip) * tab_part, width) for trip in trips],
        rep_ins,
        "rep_sum",
    )
    if n_z == 4:
        z_in = to_z(z_outs[1], 1)

        def z_half_body(spot, own_ref, in_ref, keep, out):
            dense = total((own_ref, in_ref), 0, rep_part)
            for n, ref in enumerate((keep, out)):
                ref[:rep_part, :] = dense
                ref[rep_part:, :] = total((own_ref, in_ref), rep_part + n * tab_part, tab_part)

        keep, out = call(
            z_half_body, [shape(z_rows, width)] * 2, (z_outs[0], z_in), "z_half_sum"
        )
        z_ins = [keep, to_z(out, 2)]
    else:
        z_ins = spread(to_z, z_outs, True)

    def cross_body(spot, own_ref, in_ref, out, done):
        _, _, c = spot
        done[...] = jnp.zeros_like(done)
        for t in range(n_z):
            cols = slice(t * width, (t + 1) * width)
            out[:, cols_of(2 * t + c, width)] = own_ref[:, cols]
            out[:, cols_of(2 * t + 1 - c, width)] = in_ref[:, cols]

    cross_emb, cross_done = call(
        cross_body,
        [shape(own_rows, 2 * n_z * width), shape(8, 128, F32)],
        (cross_own, cross_in),
        "cross_rows",
    )

    def z_body(spot, _, *refs):
        refs[-1][...] = total(refs[:-1], 0, z_rows)

    (mine,) = call(z_body, [shape(z_rows, width)], (cross_done, *z_ins), "z_sum")

    pieces = spread(to_rep, [mine] * n_rep)

    def gather_body(spot, *refs):
        r, _, _ = spot
        for j in range(n_rep):
            refs[n_rep][rows_of(r ^ j, dense_part), :] = refs[j][:dense_part, :]

    (dense_own,) = call(gather_body, [shape(n_rep * dense_part, width)], pieces, "dense_gather")
    dense_other = swap(dense_own)

    def table_last_body(spot, *refs):
        ins = refs[:n_rep]
        emb_ref, v_ref, g_table, g_v, g_u, g_wide, g_rows, stack, small = refs[n_rep:]
        r, z, _ = spot
        for j in range(n_rep):
            rows = slice(rep_part, rep_part + u_part)
            g_u[rows_of(r ^ j, u_part), :] = ins[j][rows, :]
            stack[rows_of(r ^ j, bag_part), :] = ins[j][rep_part + u_part :, :]
            small[rows_of(r ^ j, small_part), :] = ins[j][dense_part:rep_part, :].astype(F32)
        bag_low = stack[:n_bag, :]
        g_v[...] = mul_tn(emb_ref[...], bag_low).astype(BF)
        direct = stack[n_bag : 2 * n_bag, :].astype(F32)
        g_table[...] = (direct + mul_nt(bag_low, v_ref[...])).astype(BF)
        for q in range(n_wide):
            g_wide[:, q * width : (q + 1) * width] = small[q * feat_rows : (q + 1) * feat_rows, :]
        g_rows[...] = jnp.zeros_like(g_rows)
        for i in range(2):
            g_rows[i : i + 1, :] = small[slots[i] : slots[i] + 1, :]
        for t in range(n_z):

            @pl.when(z == t)
            def _():
                g_rows[2:3, :] = small[slots[2 + t] : slots[2 + t] + 1, :]

    grad_table, grad_v, grad_u, g_wide, g_rows = call(
        table_last_body,
        [
            shape(n_bag, width),
            shape(width, width),
            shape(width, width),
            shape(feat_rows, hidden, F32),
            shape(8, width, F32),
        ],
        (*pieces, emb_rows[0], v_emb),
        "table_last",
        [pltpu.VMEM((bag_full, width), BF), pltpu.VMEM((small_rows, width), F32)],
    )
    g_wide, g_rows = g_wide.astype(BF), g_rows.astype(BF)

    def dense_last_body(spot, own_ref, other_ref, g_second, g_vb, g_ub, stack):
        _, _, c = spot
        stack[rows_of(c, n_rep * dense_part), :] = own_ref[...]
        stack[rows_of(1 - c, n_rep * dense_part), :] = other_ref[...]
        g_second[...] = stack[:hidden, :]
        g_vb[...] = stack[hidden : hidden + width, :]
        g_ub[...] = stack[hidden + width : dense_rows, :]

    grad_ws, grad_vb, grad_ub = call(
        dense_last_body,
        [shape(hidden, width), shape(width, width), shape(width, width)],
        (dense_own, dense_other),
        "dense_last",
        [pltpu.VMEM((2 * n_rep * dense_part, width), BF)],
    )
    return (
        cross_emb,
        cross_bot,
        grad_table[None],
        grad_v,
        grad_u,
        g_rows[2],
        grad_vb,
        grad_ub,
        g_rows[1],
        g_wide[:n_feat],
        g_wide[n_feat],
        grad_ws,
        g_rows[0],
    )


def solution(mesh):
    n_rep, n_mp = mesh.devices.shape
    mesh = Mesh(mesh.devices.reshape(n_rep, n_mp // 2, 2), ("rep", "z", "core"))
    return jax.shard_map(
        local,
        mesh=mesh,
        in_specs=(
            P(("rep", "z", "core"), None),
            P("rep", ("z", "core"), None),
            P(("z", "core"), None, None),
            P(("z", "core"), None),
            P(None, ("z", "core")),
            P(("z", "core")),
            P(),
            P(),
            P(),
            P(),
            P(),
            P(),
            P(),
            P(("rep", "z", "core"), None),
            P(("rep", "z", "core"), None),
        ),
        out_specs=(
            P(("rep", "z", "core"), None),
            P(("rep", "z", "core"), None),
            P(("z", "core"), None, None),
            P(("z", "core"), None),
            P(None, ("z", "core")),
            P(("z", "core")),
            P(),
            P(),
            P(),
            P(),
            P(),
            P(),
            P(),
        ),
        check_vma=False,
    )
```

```python
import math

import jax
import jax.numpy as jnp
from jax import lax
from jax.experimental import pallas as pl
from jax.experimental.pallas import tpu as pltpu
from jax.sharding import Mesh
from jax.sharding import PartitionSpec as P

BF = jnp.bfloat16
F32 = jnp.float32
TILE = 16


def round_up(value, unit):
    return -(-value // unit) * unit


def silu_parts(inputs):
    gate_value = jax.nn.sigmoid(inputs)
    return inputs * gate_value, gate_value * (1.0 + inputs * (1.0 - gate_value))


def mul_nn(left, right):
    return lax.dot_general(left, right, (((1,), (0,)), ((), ())), preferred_element_type=F32)


def mul_tn(left, right):
    return lax.dot_general(left, right, (((0,), (0,)), ((), ())), preferred_element_type=F32)


def mul_nt(left, right):
    return lax.dot_general(left, right, (((1,), (1,)), ((), ())), preferred_element_type=F32)


def tree_sum(values):
    while len(values) > 1:
        values = [a + b for a, b in zip(values[::2], values[1::2])]
    return values[0]


def rows_of(index, count):
    return pl.ds(pl.multiple_of(index * count, TILE), count)


def cols_of(index, count):
    return pl.ds(pl.multiple_of(index * count, 128), count)


def run(body, out_shapes, args, name, scratch=(), flops=10**8, limit=6):
    in_vmem = pl.BlockSpec(memory_space=pltpu.VMEM)
    moved = sum(math.prod(a.shape) * a.dtype.itemsize for a in (*args, *out_shapes))

    def placed(spot_ref, *refs):
        body((spot_ref[0, 0], spot_ref[1, 0], spot_ref[2, 0]), *refs)

    return pl.pallas_call(
        placed,
        out_shape=out_shapes,
        in_specs=[in_vmem] * len(args),
        out_specs=[in_vmem] * len(out_shapes),
        scratch_shapes=list(scratch),
        compiler_params=pltpu.CompilerParams(vmem_limit_bytes=limit * 2**20),
        cost_estimate=pl.CostEstimate(flops=flops, bytes_accessed=moved, transcendentals=0),
        name=name,
    )(*args)


def shape(rows, cols, dtype=BF):
    return jax.ShapeDtypeStruct((rows, cols), dtype)


def local(
    dense_feats,
    bag_counts,
    emb_rows,
    v_emb,
    u_emb,
    b_emb,
    v_bot,
    u_bot,
    b_bot,
    w_first,
    b_first,
    w_second,
    b_second,
    cot_cross,
    cot_bottom,
):
    n_rep, n_z = lax.axis_size("rep"), lax.axis_size("z")
    own_rows, n_feat = dense_feats.shape
    hidden = w_first.shape[1]
    width = v_bot.shape[0]
    n_bag = bag_counts.shape[2]
    pair = 2 * own_rows
    grad_scale = 1.0 / math.sqrt(own_rows * 2 * n_z * n_rep)
    u_part = width // n_rep
    bag_part = round_up(-(-2 * n_bag // n_rep), TILE)
    bag_full = bag_part * n_rep
    dense_rows = hidden + 2 * width
    dense_part = round_up(-(-dense_rows // (2 * n_rep)), TILE)
    feat_rows = round_up(n_feat + 1, TILE)
    n_wide = hidden // width
    slots = [(q * feat_rows + i) for i in range(n_feat + 1, feat_rows) for q in range(n_wide)]
    small_rows = n_wide * feat_rows
    while len(slots) < 2 + n_z:
        slots += list(range(small_rows, small_rows + TILE))
        small_rows += TILE
    small_rows = round_up(small_rows, TILE * n_rep)
    small_part = small_rows // n_rep
    rep_part = dense_part + small_part
    half = rep_part * n_rep
    tab_part = u_part + bag_part
    z_rows = rep_part + tab_part
    msg_rows = 3 * n_bag + TILE
    gb_rows = round_up(n_z, 8)

    def swap(value):
        return lax.ppermute(value, "core", [(0, 1), (1, 0)])

    def to_z(value, k):
        return lax.ppermute(value, "z", [(i, i ^ k) for i in range(n_z)])

    def to_rep(value, k):
        return lax.ppermute(value, "rep", [(i, i ^ k) for i in range(n_rep)])

    def spread(send, values, near_first=False):
        order = range(1, len(values))
        got = {k: send(values[k], k) for k in (order if near_first else reversed(order))}
        return [values[0]] + [got[k] for k in order]

    def call(body, out_shapes, args, name, scratch=(), **options):
        return run(body, out_shapes, (spots, *args), name, scratch, **options)

    spots = jnp.stack([lax.axis_index(name) for name in ("rep", "z", "core")]).astype(jnp.int32)
    spots = jnp.broadcast_to(jnp.pad(spots, (0, 5))[:, None], (8, 128))

    def cut_body(spot, u_ref, out):
        out[...] = u_ref[rows_of(spot[0], u_part), :]

    (u_mine,) = call(cut_body, [shape(u_part, width)], (u_emb,), "u_cut", flops=2 * 10**10)
    u_z = spread(to_z, [u_mine] * n_z, True)[1:]

    def u_body(spot, *refs):
        for k, ref in enumerate(refs[:-1]):
            refs[-1][k * u_part : (k + 1) * u_part, :] = ref[...]

    (u_z,) = call(u_body, [shape((n_z - 1) * u_part, width)], u_z, "u_rows")
    u_r = spread(to_rep, [u_z] * n_rep)

    bias_rows = jnp.concatenate(
        [b[None].astype(F32) for b in (b_second, b_bot)] + [jnp.zeros((6, width), F32)]
    )

    def bags_body(spot, ct_ref, emb_ref, v_ref, b_ref, *outs):
        _, z, c = spot
        emb = emb_ref[...]
        emb_v = mul_nn(emb, v_ref[...]).astype(BF)
        bias = b_ref[...]
        for k, out in enumerate(outs):
            first = (z ^ k) * 2
            out[:n_bag, :own_rows] = ct_ref[:, cols_of(first + c, own_rows)].astype(F32).astype(BF)
            out[:n_bag, own_rows:] = (
                ct_ref[:, cols_of(first + 1 - c, own_rows)].astype(F32).astype(BF)
            )
            out[n_bag : 2 * n_bag, :] = emb
            out[2 * n_bag : 3 * n_bag, :] = emb_v
            out[3 * n_bag :, :] = bias

    counts_t = jnp.transpose(bag_counts, (1, 2, 0))[0]
    bags = call(
        bags_body,
        [shape(msg_rows, pair)] * n_z,
        (counts_t, emb_rows[0], v_emb, jnp.broadcast_to(b_emb[None], (TILE, width))),
        "bags",
    )
    bags = spread(to_z, bags, True)

    def cot_body(spot, cot_ref, out):
        _, _, c = spot
        for t in range(n_z):
            out[:, t * width : (t + 1) * width] = cot_ref[:, cols_of(2 * t + 1 - c, width)]

    (cot_out,) = call(cot_body, [shape(own_rows, n_z * width)], (cot_cross,), "cot_send")
    cot_in = swap(cot_out)

    feats_t = jnp.concatenate(
        [
            dense_feats.T,
            jnp.ones((1, own_rows), BF),
            jnp.zeros((feat_rows - n_feat - 1, own_rows), BF),
        ]
    )
    first_rows = jnp.concatenate(
        [w_first, b_first[None], jnp.zeros((feat_rows - n_feat - 1, hidden), BF)]
    )

    def mlp_body(
        spot, x_ref, w1_ref, w2_ref, b_ref, vb_ref, ub_ref, cot_ref,
        act_ref, slope1_ref, bottom_ref, slope2_ref, term_ref, back_ref,
    ):
        act, slope1_ref[...] = silu_parts(mul_tn(x_ref[...], w1_ref[...]))
        act = act.astype(BF)
        act_ref[...] = act
        bottom, slope2_ref[...] = silu_parts(mul_nn(act, w2_ref[...]) + b_ref[0:1, :])
        bottom = bottom.astype(BF)
        bottom_ref[...] = bottom
        term_ref[...] = mul_nn(bottom, vb_ref[...])
        d_lift = (cot_ref[...].astype(F32) * bottom.astype(F32)).astype(BF)
        back_ref[...] = mul_nt(d_lift, ub_ref[...])

    act, slope1, bottom, slope2, bot_term, bot_back = call(
        mlp_body,
        [
            shape(own_rows, hidden),
            shape(own_rows, hidden, F32),
            shape(own_rows, width),
            shape(own_rows, width, F32),
            shape(own_rows, width, F32),
            shape(own_rows, width, F32),
        ],
        (feats_t, first_rows, w_second, bias_rows, v_bot, u_bot, cot_bottom),
        "mlp_forward",
    )

    def part_body(spot, *refs):
        bag, u_refs = refs[:n_z], refs[n_z + 1 : n_z + 1 + n_rep]
        own_u, refs = refs[n_z], refs[n_z + 1 + n_rep :]
        cot_ref, cot_in_ref, term_ref, back_ref = refs[:4]
        part_ref, pooled_ref, lift_ref, u_ref, gb_ref = refs[4:]
        r, z, c = spot
        u_ref[:width, :] = own_u[...]
        for k in range(1, n_z):
            for j in range(n_rep):
                start = pl.multiple_of(k * width + (r ^ j) * u_part, TILE)
                u_ref[pl.ds(start, u_part), :] = u_refs[j][(k - 1) * u_part : k * u_part, :]
        low = jnp.zeros((pair, width), F32)
        back = jnp.zeros((pair, width), F32)
        gb_ref[...] = jnp.zeros_like(gb_ref)
        for k in range(n_z):
            rows = slice(k * width, (k + 1) * width)
            counts = bag[k][:n_bag, :]
            pooled = mul_tn(counts, bag[k][n_bag : 2 * n_bag, :]).astype(BF)
            low += mul_tn(counts, bag[k][2 * n_bag : 3 * n_bag, :])
            pooled_ref[rows, :] = pooled
            cot = jnp.concatenate(
                [cot_ref[:, cols_of(2 * (z ^ k) + c, width)], cot_in_ref[:, cols_of(z ^ k, width)]],
                axis=0,
            )
            d_lift = cot.astype(F32) * pooled.astype(F32)
            gb_ref[k : k + 1, :] = jnp.sum(d_lift, axis=0, keepdims=True) * grad_scale
            d_lift = d_lift.astype(BF)
            lift_ref[rows, :] = d_lift
            back += mul_nt(d_lift, u_ref[rows, :])
        part_ref[:own_rows, :] = (low[:own_rows] + term_ref[...]).astype(BF)
        part_ref[own_rows:pair, :] = low[own_rows:].astype(BF)
        part_ref[pair : pair + own_rows, :] = (back[:own_rows] + back_ref[...]).astype(BF)
        part_ref[pair + own_rows :, :] = back[own_rows:].astype(BF)

    part, pooled, d_lift, u_all, grad_b = call(
        part_body,
        [
            shape(2 * pair, width),
            shape(n_z * pair, width),
            shape(n_z * pair, width),
            shape(n_z * width, width),
            shape(gb_rows, width, F32),
        ],
        (*bags, u_emb, *u_r, cot_cross, cot_in, bot_term, bot_back),
        "partials",
    )
    part_in = swap(part)

    def summed(part_ref, in_ref, start):
        mid, end = start + own_rows, start + pair
        own = part_ref[start:mid, :].astype(F32) + in_ref[mid:end, :].astype(F32)
        other = part_ref[mid:end, :].astype(F32) + in_ref[start:mid, :].astype(F32)
        return own.astype(BF), other.astype(BF)

    def dense_body(
        spot, part_ref, in_ref, act_ref, slope1_ref, bottom_ref, slope2_ref, cot_ref, x_ref,
        w2_ref, vb_ref, ub_ref, b_ref, gb_ref,
        cross_ref, send_ref, keep_ref, pack, small,
    ):
        _, z, c = spot
        low, _ = summed(part_ref, in_ref, 0)
        d_low, _ = summed(part_ref, in_ref, pair)
        bottom = bottom_ref[...]
        bottom_full = bottom.astype(F32)
        cot = cot_ref[...].astype(F32)
        lift = mul_nn(low, ub_ref[...]) + b_ref[1:2, :] + 1.0
        cross_ref[...] = (bottom_full * lift).astype(BF)
        d_second = (cot * lift + mul_nt(d_low, vb_ref[...])) * slope2_ref[...]
        d_second_round = d_second.astype(BF)
        d_first = mul_nt(d_second_round, w2_ref[...]) * slope1_ref[...]
        d_bias = cot * bottom_full
        if 2 * n_rep * dense_part > dense_rows:
            pack[...] = jnp.zeros_like(pack)

        def put(first, value):
            value = (value * grad_scale).astype(BF)
            at, last = first, first + value.shape[0]
            while at < last:
                block = at // dense_part
                end = min(last, (block + 1) * dense_part)
                start = block * rep_part + at - block * dense_part
                pack[start : start + end - at, :] = value[at - first : end - first]
                at = end

        put(0, mul_tn(act_ref[...], d_second_round))
        put(hidden, mul_tn(bottom, d_low))
        put(hidden + width, mul_tn(low, d_bias.astype(BF)))
        small[...] = jnp.zeros_like(small)
        g_first = mul_nn(x_ref[...], d_first.astype(BF)) * grad_scale
        for q in range(n_wide):
            small[q * feat_rows : (q + 1) * feat_rows, :] = g_first[
                :, q * width : (q + 1) * width
            ]
        small[slots[0] : slots[0] + 1, :] = jnp.sum(d_second, axis=0, keepdims=True) * grad_scale
        small[slots[1] : slots[1] + 1, :] = jnp.sum(d_bias, axis=0, keepdims=True) * grad_scale
        for slot in slots[2:]:
            small[slot : slot + 1, :] = jnp.zeros((1, width), F32)

        def put_small(which):
            for j in range(n_rep):
                start = pl.multiple_of((which * n_rep + j) * rep_part + dense_part, TILE)
                pack[pl.ds(start, small_part), :] = small[
                    j * small_part : (j + 1) * small_part, :
                ].astype(BF)

        put_small(1 - c)
        send_ref[...] = pack[rows_of(1 - c, half), :]
        for k in range(n_z):
            for t in range(n_z):

                @pl.when((z ^ k) == t)
                def _():
                    small[slots[2 + t] : slots[2 + t] + 1, :] = gb_ref[k : k + 1, :]

        put_small(c)
        keep_ref[...] = pack[rows_of(c, half), :]

    cross_bot, dense_out, dense_keep = call(
        dense_body,
        [shape(own_rows, width), shape(half, width), shape(half, width)],
        (
            part, part_in, act, slope1, bottom, slope2, cot_bottom, feats_t,
            w_second, v_bot, u_bot, bias_rows, grad_b,
        ),
        "dense_grads",
        [pltpu.VMEM((2 * half, width), BF), pltpu.VMEM((small_rows, width), F32)],
    )
    dense_in = swap(dense_out)

    def table_body(spot, *refs):
        bag = refs[:n_z]
        u_ref, part_ref, in_ref, pooled_ref, lift_ref, cot_ref, cot_in_ref = refs[n_z : n_z + 7]
        own_ref, send_ref, g_u, out = refs[n_z + 7 :]
        _, z, c = spot
        low = jnp.concatenate(summed(part_ref, in_ref, 0), axis=0)
        d_low = jnp.concatenate(summed(part_ref, in_ref, pair), axis=0)
        if bag_full > 2 * n_bag:
            out[...] = jnp.zeros_like(out)
        for k in range(n_z):
            base = k * width
            counts = bag[k][:n_bag, :]
            bias = bag[k][3 * n_bag :, :].astype(F32)[0:1]
            lift = mul_nn(low, u_ref[base : base + width, :]) + bias + 1.0
            cross = (pooled_ref[base : base + width, :].astype(F32) * lift).astype(BF)
            own_ref[:, cols_of(z ^ k, width)] = cross[:own_rows]
            send_ref[:, cols_of(z ^ k, width)] = cross[own_rows:]
            cot = jnp.concatenate(
                [cot_ref[:, cols_of(2 * (z ^ k) + c, width)], cot_in_ref[:, cols_of(z ^ k, width)]],
                axis=0,
            )
            direct = (cot.astype(F32) * lift).astype(BF)
            g_u[base : base + width, :] = (
                mul_tn(low, lift_ref[base : base + width, :]) * grad_scale
            ).astype(BF)
            start = k * bag_full
            out[start : start + n_bag, :] = (mul_nn(counts, d_low) * grad_scale).astype(BF)
            out[start + n_bag : start + 2 * n_bag, :] = (
                mul_nn(counts, direct) * grad_scale
            ).astype(BF)

    cross_own, cross_out, u_keep, bag_keep = call(
        table_body,
        [shape(own_rows, n_z * width)] * 2
        + [shape(n_z * width, width), shape(n_z * bag_full, width)],
        (*bags, u_all, part, part_in, pooled, d_lift, cot_cross, cot_in),
        "table_grads",
    )

    rep_rows = rep_part + n_z * tab_part
    cut = round_up(rep_rows // 2, TILE) - TILE if n_rep == 4 else rep_rows
    if n_rep == 4:
        homes = {
            (0, 0): (0, 0), (2, 0): (0, cut), (1, 0): (1, 0), (3, 0): (1, cut),
            (0, 1): (2, 0), (1, 1): (2, rep_rows - cut), (2, 1): (3, 0), (3, 1): (3, rep_rows - cut),
        }
        pair_shapes = [shape(2 * cut, width)] * 2 + [shape(2 * (rep_rows - cut), width)] * 2
    else:
        homes = {(j, 0): (j, 0) for j in range(n_rep)}
        pair_shapes = [shape(rep_rows, width)] * n_rep

    def pair_body(spot, keep_ref, in_ref, u_ref, bag_ref, *outs):
        r, _, _ = spot

        def put(j, first, value):
            last = first + value.shape[0]
            for part, (low, high) in enumerate(((0, cut), (cut, rep_rows))):
                start, end = max(first, low), min(last, high)
                if start < end:
                    which, base = homes[j, part]
                    outs[which][base + start - low : base + end - low, :] = value[
                        start - first : end - first
                    ]

        for j in range(n_rep):
            rows = rows_of(r ^ j, rep_part)
            put(j, 0, (keep_ref[rows, :].astype(F32) + in_ref[rows, :].astype(F32)).astype(BF))
            for k in range(n_z):
                start = rep_part + k * tab_part
                rows = pl.ds(pl.multiple_of(k * width + (r ^ j) * u_part, TILE), u_part)
                put(j, start, u_ref[rows, :])
                rows = pl.ds(pl.multiple_of(k * bag_full + (r ^ j) * bag_part, TILE), bag_part)
                put(j, start + u_part, bag_ref[rows, :])

    outs = call(pair_body, pair_shapes, (dense_keep, dense_in, u_keep, bag_keep), "pair_sum")

    def total(refs, first, count):
        return tree_sum([ref[first : first + count, :].astype(F32) for ref in refs]).astype(BF)

    if n_rep == 4:
        one_in, two_in = to_rep(outs[1], 1), to_rep(outs[3], 2)

        def half_body(spot, one_ref, one_in_ref, two_ref, two_in_ref, keep, one_out, two_out):
            rest = rep_rows - cut
            keep[:cut, :] = total((one_ref, one_in_ref), 0, cut)
            one_out[...] = total((one_ref, one_in_ref), cut, cut)
            keep[cut:, :] = total((two_ref, two_in_ref), 0, rest)
            two_out[...] = total((two_ref, two_in_ref), rest, rest)

        keep, one_out, two_out = call(
            half_body,
            [shape(rep_rows, width), shape(cut, width), shape(rep_rows - cut, width)],
            (outs[0], one_in, outs[2], two_in),
            "half_sum",
        )
        rep_ins = [keep, to_rep(one_out, 2), to_rep(two_out, 1)]
    else:
        rep_ins = spread(to_rep, outs)
    cross_in = swap(cross_out)

    def rep_body(spot, *refs):
        ins, outs = refs[: len(rep_ins)], refs[len(rep_ins) :]

        def rows_sum(first, count):
            if n_rep != 4:
                return [total(ins, first, count)]
            parts = []
            if first < cut:
                parts.append(total(ins[:2], first, min(count, cut - first)))
            if first + count > cut:
                start, end = max(first, cut), first + count
                kept = ins[0][start:end, :].astype(F32)
                parts.append((kept + ins[2][start - cut : end - cut, :].astype(F32)).astype(BF))
            return parts

        def put(out, at, parts):
            for value in parts:
                out[at : at + value.shape[0], :] = value
                at += value.shape[0]

        dense = rows_sum(0, rep_part)
        for i, out in enumerate(outs):
            put(out, 0, dense)
            for n, k in enumerate(trips[i]):
                put(out, rep_part + n * tab_part, rows_sum(rep_part + k * tab_part, tab_part))

    trips = [(0, 2), (1, 3)] if n_z == 4 else [(k,) for k in range(n_z)]
    z_outs = call(
        rep_body,
        [shape(rep_part + len(trip) * tab_part, width) for trip in trips],
        rep_ins,
        "rep_sum",
    )
    if n_z == 4:
        z_in = to_z(z_outs[1], 1)

        def z_half_body(spot, own_ref, in_ref, keep, out):
            dense = total((own_ref, in_ref), 0, rep_part)
            for n, ref in enumerate((keep, out)):
                ref[:rep_part, :] = dense
                ref[rep_part:, :] = total((own_ref, in_ref), rep_part + n * tab_part, tab_part)

        keep, out = call(
            z_half_body, [shape(z_rows, width)] * 2, (z_outs[0], z_in), "z_half_sum"
        )
        z_ins = [keep, to_z(out, 2)]
    else:
        z_ins = spread(to_z, z_outs, True)

    def cross_body(spot, own_ref, in_ref, out, done):
        _, _, c = spot
        done[...] = jnp.zeros_like(done)
        for t in range(n_z):
            cols = slice(t * width, (t + 1) * width)
            out[:, cols_of(2 * t + c, width)] = own_ref[:, cols]
            out[:, cols_of(2 * t + 1 - c, width)] = in_ref[:, cols]

    cross_emb, cross_done = call(
        cross_body,
        [shape(own_rows, 2 * n_z * width), shape(8, 128, F32)],
        (cross_own, cross_in),
        "cross_rows",
    )

    def z_body(spot, _, *refs):
        refs[-1][...] = total(refs[:-1], 0, z_rows)

    (mine,) = call(z_body, [shape(z_rows, width)], (cross_done, *z_ins), "z_sum")

    pieces = spread(to_rep, [mine] * n_rep)

    others = [swap(piece) for piece in pieces]

    def small_last_body(spot, *refs):
        ins = refs[:n_rep]
        g_wide, g_bias, g_rows, small = refs[n_rep:]
        r, z, _ = spot
        for j in range(n_rep):
            small[rows_of(r ^ j, small_part), :] = ins[j][dense_part:rep_part, :].astype(F32)
        for q in range(n_wide):
            cols, start = slice(q * width, (q + 1) * width), q * feat_rows
            g_wide[:, cols] = small[start : start + n_feat, :].astype(BF)
            g_bias[:, cols] = small[start + n_feat : start + n_feat + 1, :]
        g_rows[...] = jnp.zeros_like(g_rows)
        for i in range(2):
            g_rows[i : i + 1, :] = small[slots[i] : slots[i] + 1, :]
        for t in range(n_z):

            @pl.when(z == t)
            def _():
                g_rows[2:3, :] = small[slots[2 + t] : slots[2 + t] + 1, :]

    g_wide, g_bias, g_rows = call(
        small_last_body,
        [shape(n_feat, hidden), shape(1, hidden, F32), shape(8, width, F32)],
        pieces,
        "small_last",
        [pltpu.VMEM((small_rows, width), F32)],
    )
    g_bias, g_rows = g_bias.astype(BF), g_rows.astype(BF)

    def last_body(spot, *refs):
        own, other = refs[:n_rep], refs[n_rep : 2 * n_rep]
        emb_ref, v_ref, g_table, g_v, g_u, g_second, g_vb, g_ub, bags_all, stack = refs[2 * n_rep :]
        r, _, c = spot
        for j in range(n_rep):
            stack[rows_of(c * n_rep + (r ^ j), dense_part), :] = own[j][:dense_part, :]
            stack[rows_of((1 - c) * n_rep + (r ^ j), dense_part), :] = other[j][:dense_part, :]
            g_u[rows_of(r ^ j, u_part), :] = own[j][rep_part : rep_part + u_part, :]
            bags_all[rows_of(r ^ j, bag_part), :] = own[j][rep_part + u_part :, :]
        g_second[...] = stack[:hidden, :]
        g_vb[...] = stack[hidden : hidden + width, :]
        g_ub[...] = stack[hidden + width : dense_rows, :]
        bag_low = bags_all[:n_bag, :]
        g_v[...] = mul_tn(emb_ref[...], bag_low).astype(BF)
        direct = bags_all[n_bag : 2 * n_bag, :].astype(F32)
        g_table[...] = (direct + mul_nt(bag_low, v_ref[...])).astype(BF)

    grad_table, grad_v, grad_u, grad_ws, grad_vb, grad_ub = call(
        last_body,
        [
            shape(n_bag, width),
            shape(width, width),
            shape(width, width),
            shape(hidden, width),
            shape(width, width),
            shape(width, width),
        ],
        (*pieces, *others, emb_rows[0], v_emb),
        "last_rows",
        [pltpu.VMEM((bag_full, width), BF), pltpu.VMEM((2 * n_rep * dense_part, width), BF)],
    )
    return (
        cross_emb,
        cross_bot,
        grad_table[None],
        grad_v,
        grad_u,
        g_rows[2],
        grad_vb,
        grad_ub,
        g_rows[1],
        g_wide,
        g_bias[0],
        grad_ws,
        g_rows[0],
    )


def solution(mesh):
    n_rep, n_mp = mesh.devices.shape
    mesh = Mesh(mesh.devices.reshape(n_rep, n_mp // 2, 2), ("rep", "z", "core"))
    return jax.shard_map(
        local,
        mesh=mesh,
        in_specs=(
            P(("rep", "z", "core"), None),
            P("rep", ("z", "core"), None),
            P(("z", "core"), None, None),
            P(("z", "core"), None),
            P(None, ("z", "core")),
            P(("z", "core")),
            P(),
            P(),
            P(),
            P(),
            P(),
            P(),
            P(),
            P(("rep", "z", "core"), None),
            P(("rep", "z", "core"), None),
        ),
        out_specs=(
            P(("rep", "z", "core"), None),
            P(("rep", "z", "core"), None),
            P(("z", "core"), None, None),
            P(("z", "core"), None),
            P(None, ("z", "core")),
            P(("z", "core")),
            P(),
            P(),
            P(),
            P(),
            P(),
            P(),
            P(),
        ),
        check_vma=False,
    )
```
